128 devices in a mesh: rows: 2 (over y_hi), vocab: 64 (over x, z, y_lo, core).
Axes of the slice: x: 4, y: 4 (y_hi: 2, y_lo: 2; y = y_hi * 2 + y_lo), z: 4, core: 2. Of those that a mesh axis runs over, the one named last changes fastest.
Arguments:
- teacher_hidden: bfloat16 [1536, 4096], P('rows'), may hold values from -240 to 240
- teacher_head: bfloat16 [4096, 81920], P(None, 'vocab'), may hold values from -0.25 to 0.25
- student_hidden: bfloat16 [1536, 3584], P('rows', 'vocab'), may hold values from -240 to 240
- student_head: bfloat16 [3584, 81920], P(None, 'vocab'), may hold values from -0.3125 to 0.3125
- token_ids: int32 [1536], P('rows'), may hold values from 0 to 81919
- response_mask: int32 [1536], P('rows'), may hold values from 0 to 1, as said below
Outputs:
- kl_loss: float32 [], replicated
- hidden_grad: bfloat16 [1536, 3584], P('rows', 'vocab')
The draws below stay inside these ranges and needn't reach their ends.
Inputs may be any that keep to these rules, and one draw needn't show every extreme that they name: `response_mask`: the last row of each aligned block of 8 rows is a response row.
All inputs are finite; a program needn't handle non-finite values.
Results may differ from the reference program's by a relative error of at most 0.0046.
Values may be sent and summed in bfloat16 or wider, within the bound.
A program may use at most 128 MiB of HBM per device.

```python
import math
import jax
import jax.numpy as jnp

DT = 4096
DS = 3584
ROWS = 1536
VOCAB = 81920


def scaled_rows(key, count, width):
    first_key, second_key = jax.random.split(key)
    values = jnp.clip(jax.random.normal(first_key, (count, width), jnp.float32), -6.0, 6.0)
    factors = jnp.exp(jax.random.uniform(second_key, (count, 1), jnp.float32, math.log(0.5), math.log(2.0)))
    return (values * factors).astype(jnp.bfloat16)


def draw_teacher_hidden(key, part):
    key = jax.random.fold_in(key, 11)
    return scaled_rows(key, ROWS, DT)


def draw_student_hidden(key, part):
    key = jax.random.fold_in(key, 23)
    return scaled_rows(key, ROWS, DS)


def draw_response_mask(key, part):
    key = jax.random.fold_in(key, 37)
    block_count = ROWS // 8
    rolls = jax.random.randint(key, (block_count, 8), 0, 8, jnp.int32)
    block_index = jax.lax.broadcasted_iota(jnp.int32, (block_count, 8), 0)
    position = jax.lax.broadcasted_iota(jnp.int32, (block_count, 8), 1)
    limit = jnp.where(block_index < block_count // 2, 1, 7)
    picked = (rolls < limit) | (position == 7)
    return picked.astype(jnp.int32).reshape(ROWS)


def plant(entries, rng, smallest, top_value):
    place = [jax.random.randint(jax.random.fold_in(rng, axis), (), 0, length) for axis, length in enumerate(entries.shape)]
    longest = entries.shape.index(max(entries.shape))
    next_to = place[:longest] + [(place[longest] + 1) % entries.shape[longest]] + place[longest + 1:]
    return entries.at[tuple(place)].set(smallest).at[tuple(next_to)].set(top_value)


def shard_levels(rng, extent, shards, least, largest):
    loudness, own = 1.0, jax.random.fold_in(rng, 6)
    for dim, blocks in shards:
        steps = jnp.exp(jax.random.uniform(jax.random.fold_in(own, dim), (blocks,), jnp.float32, least / len(shards), largest / len(shards)))
        loudness = loudness * jnp.repeat(steps, extent[dim] // blocks).reshape([-1 if axis == dim else 1 for axis in range(len(extent))])
    return loudness


def centred(rng, dims, spread, most, cuts=(), held_as=jnp.bfloat16):
    level = shard_levels(rng, dims, cuts, -0.22, 0.18) if cuts else 1.0
    array = jax.random.normal(rng, dims, jnp.float32) * spread * level
    return jnp.minimum(jnp.maximum(array, -most), most).astype(held_as)


def setup_inputs(seed: int = 0) -> dict:
    arg_keys = jax.random.split(jax.random.key(seed), 7)
    return {
        "teacher_hidden": draw_teacher_hidden(jax.random.fold_in(arg_keys[6], 71), 0),
        "teacher_head": centred(arg_keys[1], (DT, VOCAB), (DT // 9) ** -0.5, 0.25, ((1, 64),)),
        "student_hidden": draw_student_hidden(jax.random.fold_in(arg_keys[6], 71), 0),
        "student_head": centred(arg_keys[3], (DS, VOCAB), (DS // 9) ** -0.5, 0.3125, ((1, 64),)),
        "token_ids": plant(jax.random.randint(arg_keys[4], (ROWS,), 0, VOCAB), jax.random.fold_in(arg_keys[4], 1), 0, VOCAB - 1).astype(jnp.int32),
        "response_mask": draw_response_mask(jax.random.fold_in(arg_keys[6], 71), 0),
    }


def log_norm(logits):
    top = jnp.max(logits, axis=1)
    return top + jnp.log(jnp.sum(jnp.exp(logits - top[:, None]), axis=1))


def reference(teacher_hidden, teacher_head, student_hidden, student_head, token_ids, response_mask):
    teacher_logits = jnp.dot(teacher_hidden, teacher_head, preferred_element_type=jnp.float32)
    student_logits = jnp.dot(student_hidden, student_head, preferred_element_type=jnp.float32)
    teacher_lse = log_norm(teacher_logits)
    student_lse = log_norm(student_logits)
    teacher_prob = jnp.exp(teacher_logits - teacher_lse[:, None])
    student_prob = jnp.exp(student_logits - student_lse[:, None])
    row_kl = jnp.sum(teacher_prob * (teacher_logits - student_logits), axis=1) - teacher_lse + student_lse
    columns = jax.lax.broadcasted_iota(jnp.int32, student_logits.shape, 1)
    chosen = columns == token_ids[:, None]
    target = jnp.sum(jnp.where(chosen, student_logits, 0.0), axis=1)
    row_nll = student_lse - target
    weights = response_mask.astype(jnp.float32)
    masked = jnp.sum(weights)
    kl_loss = jnp.sum(weights * (row_kl + 0.5 * row_nll)) / masked
    row_scale = weights / masked
    logit_grad = (row_scale[:, None] * (1.5 * student_prob - teacher_prob - 0.5 * chosen.astype(jnp.float32))).astype(jnp.bfloat16)
    hidden_grad = jax.lax.dot_general(logit_grad, student_head, (((1,), (1,)), ((), ())), preferred_element_type=jnp.float32)
    return kl_loss, hidden_grad.astype(jnp.bfloat16)
```

```python
import functools

import jax
import jax.numpy as jnp
from jax import lax
from jax.experimental import pallas as pl
from jax.experimental.pallas import tpu as pltpu
from jax.sharding import PartitionSpec as P

CE_WEIGHT = 0.5
F32, BF16 = jnp.float32, jnp.bfloat16
VMEM = pl.BlockSpec(memory_space=pltpu.VMEM)
ANY = pl.BlockSpec(memory_space=pl.ANY)
DMA = pltpu.SemaphoreType.DMA
LIMIT = 60 * 2**20


class Place:
    def __init__(self):
        v = lax.axis_index("vocab")
        self.x, self.z, self.y, self.c = v // 16, (v // 4) % 4, (v // 2) % 2, v % 2
        self.row = lax.axis_index("rows")

    def at(self, dx=0, dz=0, flip_y=False, flip_c=False):
        x, z = (self.x + dx) % 4, (self.z + dz) % 4
        y = 1 - self.y if flip_y else self.y
        c = 1 - self.c if flip_c else self.c
        return {"vocab": ((x * 4 + z) * 2 + y) * 2 + c}

    def peers(self):
        return (
            [self.at(dx=d) for d in (1, 2, 3)]
            + [self.at(dz=d) for d in (1, 2, 3)]
            + [self.at(flip_y=True), self.at(flip_c=True)]
        )

    def each_core(self, step):
        for core in (0, 1):
            pl.when(self.c == core)(functools.partial(step, core))

    def lead(self, core, d):
        return self.at(dx=d) if core == 0 else self.at(dz=d)

    def other(self, core, d):
        return self.at(dz=d) if core == 0 else self.at(dx=d)

    def own(self, core):
        return (self.x, self.z) if core == 0 else (self.z, self.x)


def piece(ref, prefix, core, p, q, y):
    x, z = (p, q) if core == 0 else (q, p)
    return ref.at[(*prefix, x, z, y)]


def send(src, dst, send_sem, recv_sem, device):
    return pltpu.make_async_remote_copy(
        src_ref=src,
        dst_ref=dst,
        send_sem=send_sem,
        recv_sem=recv_sem,
        device_id=device,
        device_id_type=pl.DeviceIdType.MESH,
    )


def greet(peers):
    barrier = pltpu.get_barrier_semaphore()
    for peer in peers:
        pl.semaphore_signal(barrier, inc=1, device_id=peer, device_id_type=pl.DeviceIdType.MESH)
    pl.semaphore_wait(barrier, len(peers))


ALL = slice(None)


class Gather:
    def __init__(self, place, ht, send_sem, recv_sem, relay_send, relay_recv):
        self.place, self.ht = place, ht
        self.sems = (send_sem, recv_sem)
        self.relay_sems = (relay_send, relay_recv)

    def slots(self, core, b):
        f, g = self.place.own(core)
        y = self.place.y
        s = (2 * b + core,)
        w = functools.partial(piece, self.ht, s, core)
        m = lambda i: i % 4
        return [
            w(f, g, 1 - y),
            w(m(f + 3), g, ALL),
            w(m(f + 2), g, ALL),
            w(m(f + 1), g, ALL),
            w(ALL, m(g + 3), ALL),
            w(ALL, m(g + 1), ALL),
            w(ALL, m(g + 2), 0),
            w(ALL, m(g + 2), 1),
        ]

    def copy(self, core, b, k):
        place = self.place
        f, g = place.own(core)
        w = functools.partial(piece, self.ht, (2 * b + core,), core)
        m = lambda i: i % 4
        src, device = [
            (w(f, g, place.y), place.at(flip_y=True)),
            (w(f, g, ALL), place.lead(core, 1)),
            (w(f, g, ALL), place.lead(core, 2)),
            (w(f, g, ALL), place.lead(core, 3)),
            (w(ALL, g, ALL), place.other(core, 1)),
            (w(ALL, g, ALL), place.other(core, 3)),
            (w(ALL, m(g + 3), 0), place.other(core, 1)),
            (w(ALL, m(g + 1), 1), place.other(core, 3)),
        ][k]
        return send(src, src, self.sems[0].at[b, k], self.sems[1].at[b, k], device)

    def relay(self, core, b, k):
        slot = self.slots(core, b)[k]
        return send(
            slot, slot, self.relay_sems[0].at[b, k], self.relay_sems[1].at[b, k], self.place.at(flip_c=True)
        )

    def start(self, b, ks):
        self.place.each_core(lambda core: [self.copy(core, b, k).start() for k in ks] and None)

    def arrive(self, b, ks, then=()):
        def step(core):
            slots = self.slots(core, b)
            for k in ks:
                send(slots[k], slots[k], self.sems[0].at[b, k], self.sems[1].at[b, k], self.place.at(flip_c=True)).wait_recv()
            for k in then:
                self.copy(core, b, k).start()
            for k in ks:
                self.relay(core, b, k).start()

        self.place.each_core(step)

    def relayed(self, b, ks=range(8)):
        def step(core):
            slots = self.slots(1 - core, b)
            for k in ks:
                send(
                    slots[k], slots[k], self.relay_sems[0].at[b, k], self.relay_sems[1].at[b, k], self.place.at(flip_c=True)
                ).wait_recv()

        self.place.each_core(step)

    def drain(self, b):
        def step(core):
            for k in range(8):
                self.copy(core, b, k).wait_send()
                self.relay(core, b, k).wait_send()

        self.place.each_core(step)


def forward_kernel(
    th_hbm, tw_hbm, hid, sw_hbm, t_out, s_out,
    th, tw, sw, ht, pair, local_sem, pair_sems, g_send, g_recv, r_send, r_recv,
):
    place = Place()
    loads = [pltpu.make_async_copy(th_hbm, th, local_sem.at[0])]
    tiles = tw.shape[0]
    for i in range(tiles):
        loads.append(pltpu.make_async_copy(tw_hbm.at[:, pl.ds(i * 256, 256)], tw.at[i], local_sem.at[1 + i]))
    loads.append(pltpu.make_async_copy(sw_hbm, sw, local_sem.at[1 + tiles]))
    for load in loads:
        load.start()
    greet(place.peers())
    swap = send(hid, pair, pair_sems.at[0], pair_sems.at[1], place.at(flip_c=True))
    swap.start()
    swap.wait()
    mine, theirs = hid[...].astype(F32), pair[...].astype(F32)
    first = place.c == 0
    both = jnp.concatenate([jnp.where(first, mine, theirs), jnp.where(first, theirs, mine)], axis=1)
    turned = both.T.astype(BF16)
    for s in range(6):
        ht[s, place.x, place.z, place.y] = turned[:, s * 128 : s * 128 + 128]
    gather = Gather(place, ht, g_send, g_recv, r_send, r_recv)
    for b in range(3):
        gather.start(b, [0])
    loads[0].wait()

    def tile(i, carry):
        pltpu.make_async_copy(tw_hbm.at[:, pl.ds(i * 256, 256)], tw.at[i], local_sem.at[1 + i]).wait()
        t_out[:, pl.ds(pl.multiple_of(i * 256, 256), 256)] = jnp.dot(th[...], tw[i], preferred_element_type=F32)

        @pl.when(i == 0)
        def _():
            lax.fori_loop(0, 3, lambda b, c: gather.arrive(b, [0], [1, 2, 3]), None)

        @pl.when(i == 1)
        def _():
            lax.fori_loop(0, 3, lambda b, c: gather.arrive(b, [1, 2, 3], [4, 5]), None)

        @pl.when(i == 3)
        def _():
            gather.arrive(0, [4, 5], [6, 7])

        @pl.when(i == 4)
        def _():
            gather.arrive(1, [4, 5], [6, 7])

        return carry

    lax.fori_loop(0, tiles, tile, None)
    loads[-1].wait()

    def block(b, carry):
        gather.arrive(b, [6, 7])
        gather.relayed(b)
        lhs = jnp.concatenate([ht[2 * b].reshape(3584, 128), ht[2 * b + 1].reshape(3584, 128)], axis=1)
        s_out[pl.ds(pl.multiple_of(b * 256, 256), 256), :] = lax.dot_general(
            lhs, sw[...], (((0,), (0,)), ((), ())), preferred_element_type=F32
        )

        @pl.when(b == 0)
        def _():
            gather.arrive(2, [4, 5], [6, 7])

        return carry

    lax.fori_loop(0, 3, block, None)
    lax.fori_loop(0, 3, lambda b, c: gather.drain(b), None)


def forward(th, tw, hid, sw):
    rows, cols = th.shape[0], tw.shape[1]
    out = jax.ShapeDtypeStruct((rows, cols), F32)
    return pl.pallas_call(
        forward_kernel,
        out_shape=(out, out),
        in_specs=[ANY, ANY, VMEM, ANY],
        out_specs=(VMEM, VMEM),
        scratch_shapes=[
            pltpu.VMEM(th.shape, BF16),
            pltpu.VMEM((cols // 256, th.shape[1], 256), BF16),
            pltpu.VMEM(sw.shape, BF16),
            pltpu.VMEM((6, 4, 4, 2, 112, 128), BF16),
            pltpu.VMEM(hid.shape, BF16),
            DMA((8,)),
            DMA((2,)),
            DMA((3, 8)),
            DMA((3, 8)),
            DMA((3, 8)),
            DMA((3, 8)),
        ],
        compiler_params=pltpu.CompilerParams(collective_id=0, has_side_effects=True, vmem_limit_bytes=LIMIT),
        name="forward",
    )(th, tw, hid, sw)


def merged(parts):
    t_max = functools.reduce(jnp.maximum, [p[0:1] for p in parts])
    s_max = functools.reduce(jnp.maximum, [p[3:4] for p in parts])
    t_w = [jnp.exp(p[0:1] - t_max) for p in parts]
    s_w = [jnp.exp(p[3:4] - s_max) for p in parts]
    t_sum = sum(w * p[1:2] for w, p in zip(t_w, parts))
    cross = sum(w * p[2:3] for w, p in zip(t_w, parts))
    s_sum = sum(w * p[4:5] for w, p in zip(s_w, parts))
    target = sum(p[5:6] for p in parts)
    return jnp.concatenate([t_max, t_sum, cross, s_max, s_sum, target, target, target], axis=0)


def stats_kernel(stats, mask, out, loss_out, hold, ex, ex_send, ex_recv, s_send, s_recv):
    place = Place()
    across = {"rows": 1 - place.row}
    greet(place.peers() + [across])
    weights = mask[...].astype(F32)
    ex[0] = jnp.broadcast_to(jnp.sum(weights, axis=1, keepdims=True), (8, 128))
    count = send(ex.at[0], ex.at[1], ex_send.at[0], ex_recv.at[0], across)
    count.start()

    def stage(k, base, size, index, devices):
        copies = [
            send(hold.at[base + index], hold.at[base + index], s_send.at[base + d], s_recv.at[base + d], devices[d - 1])
            for d in range(1, size)
        ]
        for copy in copies:
            copy.start()
        for d in range(1, size):
            slot = hold.at[base + (index + size - d) % size]
            send(slot, slot, s_send.at[base + d], s_recv.at[base + d], devices[d - 1]).wait_recv()
        total = merged([hold[base + i] for i in range(size)])
        return total, copies

    hold[place.c] = stats[...]
    total, sent0 = stage(0, 0, 2, place.c, [place.at(flip_c=True)])
    hold[2 + place.y] = total
    total, sent1 = stage(1, 2, 2, place.y, [place.at(flip_y=True)])
    hold[4 + place.x] = total
    total, sent2 = stage(2, 4, 4, place.x, [place.at(dx=d) for d in (1, 2, 3)])
    hold[8 + place.z] = total
    total, sent3 = stage(3, 8, 4, place.z, [place.at(dz=d) for d in (1, 2, 3)])
    for copy in sent0 + sent1 + sent2 + sent3:
        copy.wait_send()
    t_lse = total[0:1] + jnp.log(total[1:2])
    s_lse = total[3:4] + jnp.log(total[4:5])
    row_kl = total[2:3] / total[1:2] - t_lse + s_lse
    row_nll = s_lse - total[5:6]
    count.wait()
    masked = ex[0] + ex[1]
    part = jnp.sum(weights * (row_kl + CE_WEIGHT * row_nll), axis=1, keepdims=True)
    ex[2] = jnp.broadcast_to(part, (8, 128))
    loss = send(ex.at[2], ex.at[3], ex_send.at[1], ex_recv.at[1], across)
    loss.start()
    scale = weights / masked[0:1, 0:1]
    out[...] = jnp.concatenate([t_lse, s_lse, scale, scale, scale, scale, scale, scale], axis=0)
    loss.wait()
    loss_out[...] = (ex[2] + ex[3]) / masked


def reduce_stats(stats, mask):
    return pl.pallas_call(
        stats_kernel,
        out_shape=(jax.ShapeDtypeStruct(stats.shape, F32), jax.ShapeDtypeStruct((8, 128), F32)),
        in_specs=[VMEM, VMEM],
        out_specs=(VMEM, VMEM),
        scratch_shapes=[
            pltpu.VMEM((12,) + stats.shape, F32),
            pltpu.VMEM((4, 8, 128), F32),
            DMA((2,)),
            DMA((2,)),
            DMA((12,)),
            DMA((12,)),
        ],
        compiler_params=pltpu.CompilerParams(collective_id=1, has_side_effects=True),
        name="stats",
    )(stats, mask)


class Scatter:
    def __init__(self, place, pb, bufs, send_sem, recv_sem):
        self.place, self.pb = place, pb
        self.rp, self.ra, self.rb, self.mid, self.rc, self.cs, self.cf, self.ry, self.db = bufs
        self.ss, self.rs = send_sem, recv_sem

    def copies(self, core, b):
        return [functools.partial(self.copy, core, b, k) for k in range(10)]

    def copy(self, core, b, k):
        place = self.place
        f, g = place.own(core)
        y, c = place.y, core
        m = lambda i: i % 4
        w = functools.partial(piece, self.pb, (b, c), core)
        out = [
            (self.pb.at[b, 1 - c], self.rp.at[b], place.at(flip_c=True)),
            (w(m(f + 2), ALL, 0), self.ra.at[b, 0], place.lead(core, 1)),
            (w(m(f + 2), ALL, 1), self.ra.at[b, 1], place.lead(core, 3)),
            (w(m(f + 1), ALL, ALL), self.rb.at[b, 0], place.lead(core, 1)),
            (w(m(f + 3), ALL, ALL), self.rb.at[b, 1], place.lead(core, 3)),
            (self.mid.at[b, m(g + 1)], self.rc.at[b, 0], place.other(core, 1)),
            (self.mid.at[b, m(g + 2)], self.rc.at[b, 1], place.other(core, 2)),
            (self.mid.at[b, m(g + 3)], self.rc.at[b, 2], place.other(core, 3)),
            (self.cs.at[b], self.ry.at[b], place.at(flip_y=True)),
            (self.db.at[b, c], self.db.at[b, c], place.at(flip_c=True)),
        ]
        src, dst, device = out[k]
        return send(src, dst, self.ss.at[b, k], self.rs.at[b, k], device)

    def start_pair(self, b):
        self.place.each_core(lambda core: self.copy(core, b, 0).start())

    def lead_far(self, b):
        def step(core):
            copies = self.copies(core, b)
            copies[0]().wait_recv()
            self.pb[b, core] = (self.pb[b, core].astype(F32) + self.rp[b].astype(F32)).astype(BF16)
            copies[1]().start()
            copies[2]().start()

        self.place.each_core(step)

    def lead_near(self, b):
        def step(core):
            copies = self.copies(core, b)
            f, g = self.place.own(core)
            for k, step_to, y in ((1, 1, 0), (2, 3, 1)):
                copies[k]().wait_recv()
                at = piece(self.pb, (b, core), core, (f + step_to) % 4, ALL, y)
                at[...] = (at[...].astype(F32) + self.ra[b, k - 1].astype(F32)).astype(BF16)
                copies[k + 2]().start()

        self.place.each_core(step)

    def second(self, b):
        def step(core):
            copies = self.copies(core, b)
            f, g = self.place.own(core)
            copies[3]().wait_recv()
            copies[4]().wait_recv()
            mine = piece(self.pb, (b, core), core, f, ALL, ALL)
            self.mid[b] = (
                mine[...].astype(F32) + self.rb[b, 0].astype(F32) + self.rb[b, 1].astype(F32)
            ).astype(BF16)
            for k in (5, 6, 7):
                copies[k]().start()

        self.place.each_core(step)

    def third(self, b):
        def step(core):
            copies = self.copies(core, b)
            f, g = self.place.own(core)
            for k in (5, 6, 7):
                copies[k]().wait_recv()
            total = self.mid.at[b, g][...].astype(F32)
            for d in range(3):
                total = total + self.rc[b, d].astype(F32)
            first = self.place.y == 0
            self.cf[b] = jnp.where(first, total[0], total[1])
            self.cs[b] = jnp.where(first, total[1], total[0]).astype(BF16)
            copies[8]().start()

        self.place.each_core(step)

    def last(self, b):
        def step(core):
            copies = self.copies(core, b)
            copies[8]().wait_recv()
            self.db[b, core] = (self.cf[b] + self.ry[b].astype(F32)).astype(BF16)
            copies[9]().start()

        self.place.each_core(step)

    def finish(self, b, out):
        def step(core):
            copies = self.copies(core, b)
            slot = self.db.at[b, 1 - core]
            send(slot, slot, self.ss.at[b, 9], self.rs.at[b, 9], self.place.at(flip_c=True)).wait_recv()
            for k, copy in enumerate(copies):
                copy().wait_send()
            whole = jnp.concatenate([self.db[b, 0].astype(F32), self.db[b, 1].astype(F32)], axis=1)
            mine = whole[core * 56 : core * 56 + 56]
            out[pl.ds(pl.multiple_of(b * 256, 256), 256), :] = mine.T.astype(BF16)

        self.place.each_core(step)


def backward_kernel(grad, sw, out, pb, rp, ra, rb, mid, rc, cs, cf, ry, db, s_send, s_recv):
    place = Place()
    greet(place.peers())
    scatter = Scatter(place, pb, (rp, ra, rb, mid, rc, cs, cf, ry, db), s_send, s_recv)

    def block(b, carry):
        rows = grad[pl.ds(pl.multiple_of(b * 256, 256), 256), :]

        def chunk(i, carry):
            part = lax.dot_general(
                sw[pl.ds(pl.multiple_of(i * 896, 896), 896), :],
                rows,
                (((1,), (1,)), ((), ())),
                preferred_element_type=F32,
            ).astype(BF16)
            pb[b, 0, i] = part[:, :128].reshape(4, 2, 112, 128)
            pb[b, 1, i] = part[:, 128:].reshape(4, 2, 112, 128)
            return carry

        lax.fori_loop(0, 4, chunk, None)
        scatter.start_pair(b)

        @pl.when(b > 0)
        def _():
            scatter.lead_far(b - 1)

        @pl.when(b > 1)
        def _():
            scatter.lead_near(b - 2)

        return carry

    lax.fori_loop(0, 3, block, None)
    scatter.lead_far(2)
    scatter.lead_near(1)
    scatter.second(0)
    scatter.lead_near(2)
    scatter.second(1)
    scatter.third(0)
    scatter.second(2)
    scatter.third(1)
    scatter.last(0)
    scatter.third(2)
    scatter.last(1)
    scatter.finish(0, out)
    scatter.last(2)
    scatter.finish(1, out)
    scatter.finish(2, out)


def backward(grad, sw):
    rows = grad.shape[0]
    return pl.pallas_call(
        backward_kernel,
        out_shape=jax.ShapeDtypeStruct((rows, 56), BF16),
        in_specs=[VMEM, VMEM],
        out_specs=VMEM,
        scratch_shapes=[
            pltpu.VMEM((3, 2, 4, 4, 2, 112, 128), BF16),
            pltpu.VMEM((3, 4, 4, 2, 112, 128), BF16),
            pltpu.VMEM((3, 2, 4, 112, 128), BF16),
            pltpu.VMEM((3, 2, 4, 2, 112, 128), BF16),
            pltpu.VMEM((3, 4, 2, 112, 128), BF16),
            pltpu.VMEM((3, 3, 2, 112, 128), BF16),
            pltpu.VMEM((3, 112, 128), BF16),
            pltpu.VMEM((3, 112, 128), F32),
            pltpu.VMEM((3, 112, 128), BF16),
            pltpu.VMEM((3, 2, 112, 128), BF16),
            DMA((3, 10)),
            DMA((3, 10)),
        ],
        compiler_params=pltpu.CompilerParams(collective_id=2, has_side_effects=True, vmem_limit_bytes=LIMIT),
        name="backward",
    )(grad, sw)


def local(teacher_hidden, teacher_head, student_hidden, student_head, token_ids, response_mask):
    shard_cols = teacher_head.shape[1]
    row_count = teacher_hidden.shape[0]
    t_logits, s_logits = forward(teacher_hidden, teacher_head, student_hidden, student_head)
    first_col = lax.axis_index("vocab") * shard_cols
    columns = first_col + lax.broadcasted_iota(jnp.int32, (row_count, shard_cols), 1)
    chosen = columns == token_ids[:, None]
    t_max, s_max = jnp.max(t_logits, axis=1), jnp.max(s_logits, axis=1)
    t_exp = jnp.exp(t_logits - t_max[:, None])
    s_exp = jnp.exp(s_logits - s_max[:, None])
    target = jnp.sum(jnp.where(chosen, s_logits, 0.0), axis=1)
    stats = jnp.stack(
        [
            t_max,
            jnp.sum(t_exp, axis=1),
            jnp.sum(t_exp * (t_logits - s_logits), axis=1),
            s_max,
            jnp.sum(s_exp, axis=1),
            target,
            target,
            target,
        ]
    )
    final, loss = reduce_stats(stats, response_mask[None, :])
    teacher_prob = jnp.exp(t_logits - final[0][:, None])
    student_prob = jnp.exp(s_logits - final[1][:, None])
    logit_grad = (
        final[2][:, None]
        * ((1.0 + CE_WEIGHT) * student_prob - teacher_prob - CE_WEIGHT * chosen.astype(F32))
    ).astype(BF16)
    return loss[0, 0], backward(logit_grad, student_head)


def solution(mesh):
    placed = (
        P("rows", None),
        P(None, "vocab"),
        P("rows", "vocab"),
        P(None, "vocab"),
        P("rows"),
        P("rows"),
    )
    return jax.shard_map(
        local, mesh=mesh, in_specs=placed, out_specs=(P(), P("rows", "vocab")), check_vma=False
    )
```

```python
import functools

import jax
import jax.numpy as jnp
from jax import lax
from jax.experimental import pallas as pl
from jax.experimental.pallas import tpu as pltpu
from jax.sharding import PartitionSpec as P

CE_WEIGHT = 0.5
F32, BF16 = jnp.float32, jnp.bfloat16
VMEM = pl.BlockSpec(memory_space=pltpu.VMEM)
ANY = pl.BlockSpec(memory_space=pl.ANY)
DMA = pltpu.SemaphoreType.DMA
LIMIT = 60 * 2**20


class Place:
    def __init__(self):
        v = lax.axis_index("vocab")
        self.x, self.z, self.y, self.c = v // 16, (v // 4) % 4, (v // 2) % 2, v % 2
        self.row = lax.axis_index("rows")

    def at(self, dx=0, dz=0, flip_y=False, flip_c=False):
        x, z = (self.x + dx) % 4, (self.z + dz) % 4
        y = 1 - self.y if flip_y else self.y
        c = 1 - self.c if flip_c else self.c
        return {"vocab": ((x * 4 + z) * 2 + y) * 2 + c}

    def peers(self):
        return (
            [self.at(dx=d, flip_y=f) for d in (1, 2, 3) for f in (False, True)]
            + [self.at(dz=d, flip_y=f) for d in (1, 2, 3) for f in (False, True)]
            + [self.at(dx=d, flip_c=True) for d in (1, 2, 3)]
            + [self.at(flip_y=True), self.at(flip_c=True)]
        )

    def each_core(self, step):
        for core in (0, 1):
            pl.when(self.c == core)(functools.partial(step, core))

    def lead(self, core, d, flip=False):
        return self.at(dx=d, flip_y=flip) if core == 0 else self.at(dz=d, flip_y=flip)

    def other(self, core, d, flip=False):
        return self.lead(1 - core, d, flip)

    def own(self, core):
        return (self.x, self.z) if core == 0 else (self.z, self.x)


def piece(ref, prefix, core, p, q, y):
    x, z = (p, q) if core == 0 else (q, p)
    return ref.at[(*prefix, x, z, y)]


def send(src, dst, send_sem, recv_sem, device):
    return pltpu.make_async_remote_copy(
        src_ref=src,
        dst_ref=dst,
        send_sem=send_sem,
        recv_sem=recv_sem,
        device_id=device,
        device_id_type=pl.DeviceIdType.MESH,
    )


ALL = slice(None)


SEVEN = ((1, False), (3, False), (0, True), (1, True), (3, True), (2, False), (2, True))


class Gather:
    def __init__(self, place, ht, send_sem, recv_sem, relay_send, relay_recv):
        self.place, self.ht = place, ht
        self.ss, self.rs, self.relay_ss, self.relay_rs = send_sem, recv_sem, relay_send, relay_recv

    def copy(self, core, b, k):
        place = self.place
        f, g = place.own(core)
        w = functools.partial(piece, self.ht, (2 * b + core,), core)
        if k < 7:
            d, flip = SEVEN[k]
            src, device = w(f, g, place.y), place.lead(core, d, flip)
        else:
            src, device = [
                (w(ALL, g, ALL), place.other(core, 1)),
                (w(ALL, g, ALL), place.other(core, 3)),
                (w(ALL, (g + 3) % 4, 0), place.other(core, 1)),
                (w(ALL, (g + 1) % 4, 1), place.other(core, 3)),
            ][k - 7]
        return send(src, src, self.ss.at[b, k], self.rs.at[b, k], device)

    def landed(self, core, b, k):
        f, g = self.place.own(core)
        w = functools.partial(piece, self.ht, (2 * b + core,), core)
        if k < 7:
            d, flip = SEVEN[k]
            slot = w((f + 4 - d) % 4, g, 1 - self.place.y if flip else self.place.y)
        else:
            slot = [w(ALL, (g + 3) % 4, ALL), w(ALL, (g + 1) % 4, ALL), w(ALL, (g + 2) % 4, 0), w(ALL, (g + 2) % 4, 1)][k - 7]
        send(slot, slot, self.ss.at[b, k], self.rs.at[b, k], self.place.at(flip_c=True)).wait_recv()

    def relay(self, core, b, k):
        f, g = self.place.own(core)
        w = functools.partial(piece, self.ht, (2 * b + core,), core)
        slot = [
            w(ALL, g, ALL),
            w(ALL, (g + 3) % 4, ALL),
            w(ALL, (g + 1) % 4, ALL),
            w(ALL, (g + 2) % 4, 0),
            w(ALL, (g + 2) % 4, 1),
        ][k]
        return send(slot, slot, self.relay_ss.at[b, k], self.relay_rs.at[b, k], self.place.at(flip_c=True))

    def first(self, b):
        def step(core):
            for k in range(7):
                self.copy(core, b, k).start()

        self.place.each_core(step)

    def plane(self, b):
        def step(core):
            for k in range(7):
                self.landed(core, b, k)
            self.copy(core, b, 7).start()
            self.copy(core, b, 8).start()
            self.relay(core, b, 0).start()

        self.place.each_core(step)

    def onward(self, b):
        def step(core):
            for k in (7, 8):
                self.landed(core, b, k)
                self.copy(core, b, k + 2).start()
                self.relay(core, b, k - 6).start()

        self.place.each_core(step)

    def whole(self, b):
        def step(core):
            for k in (9, 10):
                self.landed(core, b, k)
                self.relay(core, b, k - 6).start()
            for k in range(5):
                self.relay(1 - core, b, k).wait_recv()

        self.place.each_core(step)

    def drain(self, b):
        def step(core):
            for k in range(11):
                self.copy(core, b, k).wait_send()
            for k in range(5):
                self.relay(core, b, k).wait_send()

        self.place.each_core(step)


def merged(parts):
    t_max = functools.reduce(jnp.maximum, [p[0:1] for p in parts])
    s_max = functools.reduce(jnp.maximum, [p[3:4] for p in parts])
    t_w = [jnp.exp(p[0:1] - t_max) for p in parts]
    s_w = [jnp.exp(p[3:4] - s_max) for p in parts]
    t_sum = sum(w * p[1:2] for w, p in zip(t_w, parts))
    cross = sum(w * p[2:3] for w, p in zip(t_w, parts))
    s_sum = sum(w * p[4:5] for w, p in zip(s_w, parts))
    target = sum(p[5:6] for p in parts)
    return jnp.concatenate([t_max, t_sum, cross, s_max, s_sum, target, target, target], axis=0)


class Statistics:
    def __init__(self, place, hold, send_sem, recv_sem):
        self.place, self.hold, self.ss, self.rs = place, hold, send_sem, recv_sem

    def copies(self, b, stage):
        place = self.place
        own = self.own(stage)
        out = []
        for k, (d, flip) in enumerate(SEVEN):
            device = place.at(dx=d, flip_c=flip) if stage == 0 else place.at(dz=d, flip_y=flip)
            slot = self.hold.at[b, stage, own]
            out.append(send(slot, slot, self.ss.at[b, stage, k], self.rs.at[b, stage, k], device))
        return out

    def own(self, stage):
        place = self.place
        return place.x * 2 + place.c if stage == 0 else place.z * 2 + place.y

    def start(self, b, stage, value):
        self.hold[b, stage, self.own(stage)] = value
        for copy in self.copies(b, stage):
            copy.start()

    def total(self, b, stage):
        place = self.place
        main, pair = (place.x, place.c) if stage == 0 else (place.z, place.y)
        for k, (d, flip) in enumerate(SEVEN):
            index = (main + 4 - d) % 4 * 2 + (1 - pair if flip else pair)
            slot = self.hold.at[b, stage, index]
            send(slot, slot, self.ss.at[b, stage, k], self.rs.at[b, stage, k], place.at(flip_c=True)).wait_recv()
        return merged([self.hold[b, stage, i] for i in range(8)])

    def drain(self, b):
        for stage in (0, 1):
            for copy in self.copies(b, stage):
                copy.wait_send()


class Scatter:
    def __init__(self, place, pb, bufs, send_sem, recv_sem):
        self.place, self.pb = place, pb
        self.rp, self.ra, self.rb, self.mid, self.rc, self.db = bufs
        self.ss, self.rs = send_sem, recv_sem

    def copy(self, core, b, k):
        place = self.place
        f, g = place.own(core)
        w = functools.partial(piece, self.pb, (b, core), core)
        if 5 <= k < 12:
            d, flip = SEVEN[k - 5]
            src = self.mid.at[b, (g + d) % 4, 1 - place.y if flip else place.y]
            dst, device = self.rc.at[b, k - 5], place.other(core, d, flip)
        else:
            src, dst, device = {
                0: lambda: (self.pb.at[b, 1 - core], self.rp.at[b], place.at(flip_c=True)),
                1: lambda: (w((f + 2) % 4, ALL, 0), self.ra.at[b, 0], place.lead(core, 1)),
                2: lambda: (w((f + 2) % 4, ALL, 1), self.ra.at[b, 1], place.lead(core, 3)),
                3: lambda: (w((f + 1) % 4, ALL, ALL), self.rb.at[b, 0], place.lead(core, 1)),
                4: lambda: (w((f + 3) % 4, ALL, ALL), self.rb.at[b, 1], place.lead(core, 3)),
                12: lambda: (self.db.at[b, core], self.db.at[b, core], place.at(flip_c=True)),
            }[k]()
        return send(src, dst, self.ss.at[b, k], self.rs.at[b, k], device)

    def start_pair(self, b):
        self.place.each_core(lambda core: self.copy(core, b, 0).start())

    def lead_far(self, b):
        def step(core):
            self.copy(core, b, 0).wait_recv()
            self.pb[b, core] = (self.pb[b, core].astype(F32) + self.rp[b].astype(F32)).astype(BF16)
            self.copy(core, b, 1).start()
            self.copy(core, b, 2).start()

        self.place.each_core(step)

    def lead_near(self, b):
        def step(core):
            f, g = self.place.own(core)
            for k, ahead, y in ((1, 1, 0), (2, 3, 1)):
                self.copy(core, b, k).wait_recv()
                at = piece(self.pb, (b, core), core, (f + ahead) % 4, ALL, y)
                at[...] = (at[...].astype(F32) + self.ra[b, k - 1].astype(F32)).astype(BF16)
                self.copy(core, b, k + 2).start()

        self.place.each_core(step)

    def second(self, b):
        def step(core):
            f, g = self.place.own(core)
            self.copy(core, b, 3).wait_recv()
            self.copy(core, b, 4).wait_recv()
            mine = piece(self.pb, (b, core), core, f, ALL, ALL)
            self.mid[b] = (mine[...].astype(F32) + self.rb[b, 0].astype(F32) + self.rb[b, 1].astype(F32)).astype(BF16)
            for k in range(5, 12):
                self.copy(core, b, k).start()

        self.place.each_core(step)

    def last(self, b):
        def step(core):
            f, g = self.place.own(core)
            for k in range(5, 12):
                self.copy(core, b, k).wait_recv()
            total = self.mid.at[b, g, self.place.y][...].astype(F32)
            for k in range(7):
                total = total + self.rc[b, k].astype(F32)
            self.db[b, core] = total.astype(BF16)
            self.copy(core, b, 12).start()

        self.place.each_core(step)

    def finish(self, b, out):
        def step(core):
            slot = self.db.at[b, 1 - core]
            send(slot, slot, self.ss.at[b, 12], self.rs.at[b, 12], self.place.at(flip_c=True)).wait_recv()
            for k in range(13):
                self.copy(core, b, k).wait_send()
            for half in (0, 1):
                mine = self.db[b, half].astype(F32)[core * 56 : core * 56 + 56]
                out[:, b * 256 + half * 128 : b * 256 + half * 128 + 128] = mine.astype(BF16)

        self.place.each_core(step)


def kernel(
    th_hbm, tw_hbm, hid, sw_hbm, tok, mask, loss_out, out,
    th, tw, sw, ht, pair, et, es, gb, info, tcol, col, coef, hold, ex, lossv, pb, rp, ra, rb, mid, rc, db,
    local_sem, pair_sems, ex_send, ex_recv, g_send, g_recv, r_send, r_recv, st_send, st_recv, s_send, s_recv,
):
    place = Place()
    across = {"rows": 1 - place.row}
    peers = place.peers() + [across]
    barrier = pltpu.get_barrier_semaphore()
    for peer in peers:
        pl.semaphore_signal(barrier, inc=1, device_id=peer, device_id_type=pl.DeviceIdType.MESH)

    th_load = lambda i: pltpu.make_async_copy(th_hbm.at[pl.ds(i * 128, 128)], th.at[pl.ds(i * 128, 128)], local_sem.at[i])
    tw_load = lambda i: pltpu.make_async_copy(
        tw_hbm.at[pl.ds(i * 1024, 1024)], tw.at[pl.ds(i * 1024, 1024)], local_sem.at[6 + i]
    )
    sw_load = lambda i: pltpu.make_async_copy(
        sw_hbm.at[pl.ds(i * 896, 896)], sw.at[pl.ds(i * 896, 896)], local_sem.at[10 + i]
    )
    th_load(0).start()
    for i in range(4):
        tw_load(i).start()
    for i in range(1, 6):
        th_load(i).start()
    for i in range(4):
        sw_load(i).start()

    mine = jnp.concatenate([hid[...].astype(F32), jnp.zeros((8, 768), F32)], axis=0).astype(BF16)
    for b in range(3):
        for half in (0, 1):
            pair[0, b, half] = mine[:, b * 256 + half * 128 : b * 256 + half * 128 + 128]
    pl.semaphore_wait(barrier, len(peers))
    swaps = [
        send(
            pair.at[0, b, 1 - place.c], pair.at[1, b, 1 - place.c], pair_sems.at[0, b], pair_sems.at[1, b], place.at(flip_c=True)
        )
        for b in range(3)
    ]
    for swap in swaps:
        swap.start()

    weights = mask[...].astype(F32).reshape(1, 768)
    ex[0] = jnp.broadcast_to(jnp.sum(weights, axis=1, keepdims=True), (8, 128))
    count = send(ex.at[0], ex.at[1], ex_send.at[0], ex_recv.at[0], across)
    count.start()
    gather = Gather(place, ht, g_send, g_recv, r_send, r_recv)

    for b in range(3):
        slot = pair.at[1, b, place.c]
        send(slot, slot, pair_sems.at[0, b], pair_sems.at[1, b], place.at(flip_c=True)).wait_recv()
        own = pair[0, b, place.c].astype(F32)[:56]
        theirs = pair[1, b, place.c].astype(F32)[:56]
        first = place.c == 0
        both = jnp.concatenate([jnp.where(first, own, theirs), jnp.where(first, theirs, own)], axis=0)
        ht[2 * b + place.c, place.x, place.z, place.y] = both.astype(BF16)
        gather.first(b)

    first_col = lax.axis_index("vocab") * 1280
    local_tok = (tok[...] - first_col).astype(F32).reshape(1, 768)
    info[...] = jnp.broadcast_to(local_tok, (128, 768)).T

    for i in range(4):
        tw_load(i).wait()

    def teacher(i, carry):
        rows = pl.ds(pl.multiple_of(i * 128, 128), 128)
        th_load(i).wait()
        et[rows, :] = jnp.dot(th[rows, :], tw[...], preferred_element_type=F32)
        pl.when(i == 2)(lambda: gather.plane(0))
        pl.when(i == 3)(lambda: gather.plane(1))
        pl.when(i == 4)(lambda: gather.plane(2))
        pl.when(i == 5)(lambda: gather.onward(0))
        return carry

    lax.fori_loop(0, 6, teacher, None)

    lane = lax.broadcasted_iota(jnp.int32, (32, 128), 1)

    def teacher_rows(i, carry):
        rows = pl.ds(pl.multiple_of(i * 32, 32), 32)
        t = et[rows, :]
        top = jnp.max(t, axis=1, keepdims=True)
        e = jnp.exp(t - top)
        et[rows, :] = e
        total = jnp.sum(e, axis=1, keepdims=True)
        mean = jnp.sum(e * t, axis=1, keepdims=True)
        tcol[rows, :] = jnp.where(lane == 0, top, jnp.where(lane == 1, total, jnp.where(lane == 2, mean, 0.0)))
        return carry

    lax.fori_loop(0, 12, teacher_rows, None)
    gather.onward(1)
    lax.fori_loop(12, 24, teacher_rows, None)
    gather.onward(2)
    for i in range(4):
        sw_load(i).wait()
    count.wait()

    stats = Statistics(place, hold, st_send, st_recv)
    column = lax.broadcasted_iota(jnp.int32, (32, 1280), 1).astype(F32)

    def student_rows(b):
        def step(i, carry):
            rows = pl.ds(pl.multiple_of(b * 256 + i * 32, 32), 32)
            s = es[rows, :]
            top = jnp.max(s, axis=1, keepdims=True)
            e = jnp.exp(s - top)
            es[rows, :] = e
            total = jnp.sum(e, axis=1, keepdims=True)
            mean = jnp.sum(et[rows, :] * s, axis=1, keepdims=True)
            target = jnp.sum(jnp.where(column == info[rows, 0:1], s, 0.0), axis=1, keepdims=True)
            old = tcol[rows, :]
            new = jnp.where(lane == 2, old - mean, old)
            new = jnp.where(lane == 3, top, jnp.where(lane == 4, total, jnp.where(lane == 5, target, new)))
            col[pl.ds(pl.multiple_of(i * 32, 32), 32), :] = new
            return carry

        lax.fori_loop(0, 8, step, None)
        stats.start(b, 0, col[...].T[:8])

    def settle(b):
        total = stats.total(b, 1)
        mine = hold[b, 0, stats.own(0)]
        t_lse = total[0:1] + jnp.log(total[1:2])
        s_lse = total[3:4] + jnp.log(total[4:5])
        row_kl = total[2:3] / total[1:2] - t_lse + s_lse
        row_nll = s_lse - total[5:6]
        masked = ex[0, 0:1, 0:1] + ex[1, 0:1, 0:1]
        weight = lossv[b, 1:2]
        lossv[b, 0:1] = weight * (row_kl + CE_WEIGHT * row_nll)
        scale = weight / masked
        a_s = (1.0 + CE_WEIGHT) * scale * jnp.exp(mine[3:4] - s_lse)
        a_t = scale * jnp.exp(mine[0:1] - t_lse)
        a_o = CE_WEIGHT * scale
        rows = jnp.concatenate([a_s, a_t, a_o, a_o, a_o, a_o, a_o, a_o], axis=0)
        coef[b] = jnp.concatenate([rows] * 16, axis=0).T

    for b in range(3):
        lossv[b, 1:2] = weights[:, b * 256 : b * 256 + 256]

    def student(b, carry):
        gather.whole(b)
        lhs = jnp.concatenate([ht[2 * b].reshape(3584, 128), ht[2 * b + 1].reshape(3584, 128)], axis=1)
        es[pl.ds(pl.multiple_of(b * 256, 256), 256), :] = lax.dot_general(
            lhs, sw[...], (((0,), (0,)), ((), ())), preferred_element_type=F32
        )
        pl.when(b >= 1)(lambda: stats.start(b - 1, 1, stats.total(b - 1, 0)))
        student_rows(b)
        pl.when(b == 2)(lambda: settle(0))
        return carry

    lax.fori_loop(0, 3, student, None)

    scatter = Scatter(place, pb, (rp, ra, rb, mid, rc, db), s_send, s_recv)

    def backward(b, carry):
        def grad_rows(i, carry):
            rows = pl.ds(pl.multiple_of(i * 32, 32), 32)
            full = pl.ds(pl.multiple_of(b * 256 + i * 32, 32), 32)
            a_s, a_t, a_o = (coef[b, rows, k : k + 1] for k in range(3))
            chosen = jnp.where(column == info[full, 0:1], a_o, 0.0)
            gb[rows, :] = (es[full, :] * a_s - et[full, :] * a_t - chosen).astype(BF16)
            return carry

        lax.fori_loop(0, 8, grad_rows, None)
        part = lax.dot_general(sw[...], gb[...], (((1,), (1,)), ((), ())), preferred_element_type=F32).astype(BF16)
        pb[b, 0] = part[:, :128].reshape(4, 4, 2, 112, 128)
        pb[b, 1] = part[:, 128:].reshape(4, 4, 2, 112, 128)
        scatter.start_pair(b)

        @pl.when(b == 0)
        def _():
            stats.start(2, 1, stats.total(2, 0))
            settle(1)

        @pl.when(b == 1)
        def _():
            scatter.lead_far(0)
            settle(2)

        @pl.when(b == 2)
        def _():
            scatter.lead_far(1)
            scatter.lead_near(0)

        return carry

    lax.fori_loop(0, 3, backward, None)
    part = lossv[0, 0:1] + lossv[1, 0:1] + lossv[2, 0:1]
    ex[2] = jnp.broadcast_to(jnp.sum(part, axis=1, keepdims=True), (8, 128))
    loss = send(ex.at[2], ex.at[3], ex_send.at[1], ex_recv.at[1], across)
    loss.start()
    scatter.lead_far(2)
    scatter.lead_near(1)
    scatter.second(0)
    scatter.lead_near(2)
    scatter.second(1)
    scatter.last(0)
    scatter.second(2)
    scatter.last(1)
    scatter.finish(0, out)
    scatter.last(2)
    scatter.finish(1, out)
    loss.wait()
    loss_out[...] = (ex[2] + ex[3]) / (ex[0] + ex[1])

    def tidy(b, carry):
        gather.drain(b)
        stats.drain(b)
        return carry

    lax.fori_loop(0, 3, tidy, None)
    for swap in swaps:
        swap.wait_send()
    scatter.finish(2, out)


def local(teacher_hidden, teacher_head, student_hidden, student_head, token_ids, response_mask):
    loss, grad = pl.pallas_call(
        kernel,
        out_shape=(jax.ShapeDtypeStruct((8, 128), F32), jax.ShapeDtypeStruct((56, 768), BF16)),
        in_specs=[ANY, ANY, VMEM, ANY, VMEM, VMEM],
        out_specs=(VMEM, VMEM),
        scratch_shapes=[
            pltpu.VMEM((768, 4096), BF16),
            pltpu.VMEM((4096, 1280), BF16),
            pltpu.VMEM((3584, 1280), BF16),
            pltpu.VMEM((6, 4, 4, 2, 112, 128), BF16),
            pltpu.VMEM((2, 3, 2, 64, 128), BF16),
            pltpu.VMEM((768, 1280), F32),
            pltpu.VMEM((768, 1280), F32),
            pltpu.VMEM((256, 1280), BF16),
            pltpu.VMEM((768, 128), F32),
            pltpu.VMEM((768, 128), F32),
            pltpu.VMEM((256, 128), F32),
            pltpu.VMEM((3, 256, 128), F32),
            pltpu.VMEM((3, 2, 8, 8, 256), F32),
            pltpu.VMEM((4, 8, 128), F32),
            pltpu.VMEM((3, 8, 256), F32),
            pltpu.VMEM((3, 2, 4, 4, 2, 112, 128), BF16),
            pltpu.VMEM((3, 4, 4, 2, 112, 128), BF16),
            pltpu.VMEM((3, 2, 4, 112, 128), BF16),
            pltpu.VMEM((3, 2, 4, 2, 112, 128), BF16),
            pltpu.VMEM((3, 4, 2, 112, 128), BF16),
            pltpu.VMEM((3, 7, 112, 128), BF16),
            pltpu.VMEM((3, 2, 112, 128), BF16),
            DMA((14,)),
            DMA((2, 3)),
            DMA((2,)),
            DMA((2,)),
            DMA((3, 11)),
            DMA((3, 11)),
            DMA((3, 5)),
            DMA((3, 5)),
            DMA((3, 2, 7)),
            DMA((3, 2, 7)),
            DMA((3, 13)),
            DMA((3, 13)),
        ],
        compiler_params=pltpu.CompilerParams(collective_id=0, has_side_effects=True, vmem_limit_bytes=LIMIT),
        name="distill",
    )(teacher_hidden, teacher_head, student_hidden.T, student_head, token_ids, response_mask)
    return loss[0, 0], grad.T


def solution(mesh):
    placed = (
        P("rows", None),
        P(None, "vocab"),
        P("rows", "vocab"),
        P(None, "vocab"),
        P("rows"),
        P("rows"),
    )
    return jax.shard_map(
        local, mesh=mesh, in_specs=placed, out_specs=(P(), P("rows", "vocab")), check_vma=False
    )
```

```python
import functools

import jax
import jax.numpy as jnp
from jax import lax
from jax.experimental import pallas as pl
from jax.experimental.pallas import tpu as pltpu
from jax.sharding import PartitionSpec as P

CE_WEIGHT = 0.5
STRIP = 64
F32, BF16 = jnp.float32, jnp.bfloat16
VMEM = pl.BlockSpec(memory_space=pltpu.VMEM)
ANY = pl.BlockSpec(memory_space=pl.ANY)
DMA = pltpu.SemaphoreType.DMA
LIMIT = 60 * 2**20


class Place:
    def __init__(self):
        v = lax.axis_index("vocab")
        self.x, self.z, self.y, self.c = v // 16, (v // 4) % 4, (v // 2) % 2, v % 2
        self.row = lax.axis_index("rows")

    def at(self, dx=0, dz=0, flip_y=False, flip_c=False):
        x, z = (self.x + dx) % 4, (self.z + dz) % 4
        y = 1 - self.y if flip_y else self.y
        c = 1 - self.c if flip_c else self.c
        return {"vocab": ((x * 4 + z) * 2 + y) * 2 + c}

    def peers(self):
        return (
            [self.at(dx=d, flip_y=f) for d in (1, 2, 3) for f in (False, True)]
            + [self.at(dz=d, flip_y=f) for d in (1, 2, 3) for f in (False, True)]
            + [self.at(dx=d, flip_c=True) for d in (1, 2, 3)]
            + [self.at(flip_y=True), self.at(flip_c=True)]
        )

    def each_core(self, step):
        for core in (0, 1):
            pl.when(self.c == core)(functools.partial(step, core))

    def lead(self, core, d, flip=False):
        return self.at(dx=d, flip_y=flip) if core == 0 else self.at(dz=d, flip_y=flip)

    def other(self, core, d, flip=False):
        return self.lead(1 - core, d, flip)

    def own(self, core):
        return (self.x, self.z) if core == 0 else (self.z, self.x)


def piece(ref, prefix, core, p, q, y):
    x, z = (p, q) if core == 0 else (q, p)
    return ref.at[(*prefix, x, z, y)]


def send(src, dst, send_sem, recv_sem, device):
    return pltpu.make_async_remote_copy(
        src_ref=src,
        dst_ref=dst,
        send_sem=send_sem,
        recv_sem=recv_sem,
        device_id=device,
        device_id_type=pl.DeviceIdType.MESH,
    )


ALL = slice(None)


SEVEN = ((1, False), (3, False), (0, True), (1, True), (3, True), (2, False), (2, True))


class Gather:
    def __init__(self, place, ht, send_sem, recv_sem, relay_send, relay_recv):
        self.place, self.ht = place, ht
        self.ss, self.rs, self.relay_ss, self.relay_rs = send_sem, recv_sem, relay_send, relay_recv

    def copy(self, core, b, k):
        place = self.place
        f, g = place.own(core)
        w = functools.partial(piece, self.ht, (2 * b + core,), core)
        src, device = [
            (w(f, g, place.y), place.at(flip_y=True)),
            (w(f, g, ALL), place.lead(core, 1)),
            (w(f, g, ALL), place.lead(core, 2)),
            (w(f, g, ALL), place.lead(core, 3)),
            (w(ALL, g, 0), place.other(core, 1)),
            (w(ALL, g, 1), place.other(core, 3)),
            (w(ALL, g, 1), place.other(core, 1)),
            (w(ALL, g, 0), place.other(core, 3)),
            (w(ALL, (g + 3) % 4, 0), place.other(core, 1)),
            (w(ALL, (g + 1) % 4, 1), place.other(core, 3)),
        ][k]
        return send(src, src, self.ss.at[b, k], self.rs.at[b, k], device)

    def landed(self, core, b, k):
        f, g = self.place.own(core)
        w = functools.partial(piece, self.ht, (2 * b + core,), core)
        slot = [
            w(f, g, 1 - self.place.y),
            w((f + 3) % 4, g, ALL),
            w((f + 2) % 4, g, ALL),
            w((f + 1) % 4, g, ALL),
            w(ALL, (g + 3) % 4, 0),
            w(ALL, (g + 1) % 4, 1),
            w(ALL, (g + 3) % 4, 1),
            w(ALL, (g + 1) % 4, 0),
            w(ALL, (g + 2) % 4, 0),
            w(ALL, (g + 2) % 4, 1),
        ][k]
        send(slot, slot, self.ss.at[b, k], self.rs.at[b, k], self.place.at(flip_c=True)).wait_recv()

    def relay(self, core, b, k):
        f, g = self.place.own(core)
        w = functools.partial(piece, self.ht, (2 * b + core,), core)
        slot = [
            w(ALL, g, ALL),
            w(ALL, (g + 3) % 4, ALL),
            w(ALL, (g + 1) % 4, ALL),
            w(ALL, (g + 2) % 4, 0),
            w(ALL, (g + 2) % 4, 1),
        ][k]
        return send(slot, slot, self.relay_ss.at[b, k], self.relay_rs.at[b, k], self.place.at(flip_c=True))

    def first(self, b):
        self.place.each_core(lambda core: self.copy(core, b, 0).start())

    def line(self, b):
        def step(core):
            self.landed(core, b, 0)
            for k in (1, 3, 2):
                self.copy(core, b, k).start()

        self.place.each_core(step)

    def plane(self, b):
        def step(core):
            for k in (1, 2, 3):
                self.landed(core, b, k)
            self.copy(core, b, 4).start()
            self.copy(core, b, 5).start()
            self.relay(core, b, 0).start()

        self.place.each_core(step)

    def plane_rest(self, b):
        def step(core):
            self.copy(core, b, 6).start()
            self.copy(core, b, 7).start()

        self.place.each_core(step)

    def onward(self, b):
        def step(core):
            for k in (4, 5):
                self.landed(core, b, k)
                self.copy(core, b, k + 4).start()

        self.place.each_core(step)

    def rest(self, b):
        def step(core):
            for k in (6, 7):
                self.landed(core, b, k)
                self.relay(core, b, k - 5).start()

        self.place.each_core(step)

    def whole(self, b):
        def step(core):
            for k in (8, 9):
                self.landed(core, b, k)
                self.relay(core, b, k - 5).start()
            for k in range(5):
                self.relay(1 - core, b, k).wait_recv()

        self.place.each_core(step)

    def drain(self, b):
        def step(core):
            for k in range(10):
                self.copy(core, b, k).wait_send()
            for k in range(5):
                self.relay(core, b, k).wait_send()

        self.place.each_core(step)


def merged(parts):
    t_max = functools.reduce(jnp.maximum, [p[0:1] for p in parts])
    s_max = functools.reduce(jnp.maximum, [p[3:4] for p in parts])
    t_w = [jnp.exp(p[0:1] - t_max) for p in parts]
    s_w = [jnp.exp(p[3:4] - s_max) for p in parts]
    t_sum = sum(w * p[1:2] for w, p in zip(t_w, parts))
    cross = sum(w * p[2:3] for w, p in zip(t_w, parts))
    s_sum = sum(w * p[4:5] for w, p in zip(s_w, parts))
    target = sum(p[5:6] for p in parts)
    return jnp.concatenate([t_max, t_sum, cross, s_max, s_sum, target, target, target], axis=0)


class Statistics:
    def __init__(self, place, hold, send_sem, recv_sem):
        self.place, self.hold, self.ss, self.rs = place, hold, send_sem, recv_sem

    def copies(self, b, stage):
        place = self.place
        own = self.own(stage)
        out = []
        for k, (d, flip) in enumerate(SEVEN):
            device = place.at(dx=d, flip_c=flip) if stage == 0 else place.at(dz=d, flip_y=flip)
            slot = self.hold.at[b, stage, own]
            out.append(send(slot, slot, self.ss.at[b, stage, k], self.rs.at[b, stage, k], device))
        return out

    def own(self, stage):
        place = self.place
        return place.x * 2 + place.c if stage == 0 else place.z * 2 + place.y

    def start(self, b, stage, value):
        self.hold[b, stage, self.own(stage)] = value
        for copy in self.copies(b, stage):
            copy.start()

    def total(self, b, stage):
        place = self.place
        main, pair = (place.x, place.c) if stage == 0 else (place.z, place.y)
        for k, (d, flip) in enumerate(SEVEN):
            index = (main + 4 - d) % 4 * 2 + (1 - pair if flip else pair)
            slot = self.hold.at[b, stage, index]
            send(slot, slot, self.ss.at[b, stage, k], self.rs.at[b, stage, k], place.at(flip_c=True)).wait_recv()
        return merged([self.hold[b, stage, i] for i in range(8)])

    def drain(self, b):
        for stage in (0, 1):
            for copy in self.copies(b, stage):
                copy.wait_send()


class Scatter:
    def __init__(self, place, pb, bufs, send_sem, recv_sem):
        self.place, self.pb = place, pb
        self.rp, self.ra, self.rb, self.mid, self.rc, self.db = bufs
        self.ss, self.rs = send_sem, recv_sem

    def copy(self, core, b, k):
        place = self.place
        f, g = place.own(core)
        w = functools.partial(piece, self.pb, (b, core), core)
        if 5 <= k < 12:
            d, flip = SEVEN[k - 5]
            src = self.mid.at[b, (g + d) % 4, 1 - place.y if flip else place.y]
            dst, device = self.rc.at[b, k - 5], place.other(core, d, flip)
        else:
            src, dst, device = {
                0: lambda: (self.pb.at[b, 1 - core, 0:2], self.rp.at[b, 0:2], place.at(flip_c=True)),
                13: lambda: (self.pb.at[b, 1 - core, 2:4], self.rp.at[b, 2:4], place.at(flip_c=True)),
                1: lambda: (w((f + 2) % 4, ALL, 0), self.ra.at[b, 0], place.lead(core, 1)),
                2: lambda: (w((f + 2) % 4, ALL, 1), self.ra.at[b, 1], place.lead(core, 3)),
                3: lambda: (w((f + 1) % 4, ALL, 1), self.rb.at[b, 0, :, 1], place.lead(core, 1)),
                4: lambda: (w((f + 3) % 4, ALL, 0), self.rb.at[b, 1, :, 0], place.lead(core, 3)),
                14: lambda: (w((f + 1) % 4, ALL, 0), self.rb.at[b, 0, :, 0], place.lead(core, 1)),
                15: lambda: (w((f + 3) % 4, ALL, 1), self.rb.at[b, 1, :, 1], place.lead(core, 3)),
                12: lambda: (self.db.at[b, core], self.db.at[b, core], place.at(flip_c=True)),
            }[k]()
        return send(src, dst, self.ss.at[b, k], self.rs.at[b, k], device)

    def start_pair(self, b, half):
        self.place.each_core(lambda core: self.copy(core, b, 13 * half).start())

    def pair_sum(self, core, b, ahead):
        f, g = self.place.own(core)
        at = piece(self.pb, (b, core), core, (f + ahead) % 4, ALL, ALL)
        theirs = piece(self.rp, (b,), core, (f + ahead) % 4, ALL, ALL)
        return at, at[...].astype(F32) + theirs[...].astype(F32)

    def lead_far(self, b):
        def step(core):
            self.copy(core, b, 0).wait_recv()
            self.copy(core, b, 13).wait_recv()
            for ahead in (2, 1, 3):
                at, value = self.pair_sum(core, b, ahead)
                at[...] = value.astype(BF16)
                for k in {2: (1, 2), 1: (3,), 3: (4,)}[ahead]:
                    self.copy(core, b, k).start()

        self.place.each_core(step)

    def lead_near(self, b):
        def step(core):
            f, g = self.place.own(core)
            for k, ahead, y in ((1, 1, 0), (2, 3, 1)):
                self.copy(core, b, k).wait_recv()
                at = piece(self.pb, (b, core), core, (f + ahead) % 4, ALL, y)
                at[...] = (at[...].astype(F32) + self.ra[b, k - 1].astype(F32)).astype(BF16)
                self.copy(core, b, k + 13).start()

        self.place.each_core(step)

    def second(self, b):
        def step(core):
            f, g = self.place.own(core)
            for k in (3, 4, 14, 15):
                self.copy(core, b, k).wait_recv()
            at, mine = self.pair_sum(core, b, 0)
            self.mid[b] = (mine + self.rb[b, 0].astype(F32) + self.rb[b, 1].astype(F32)).astype(BF16)
            for k in range(5, 12):
                self.copy(core, b, k).start()

        self.place.each_core(step)

    def last(self, b):
        def step(core):
            f, g = self.place.own(core)
            for k in range(5, 12):
                self.copy(core, b, k).wait_recv()
            total = self.mid.at[b, g, self.place.y][...].astype(F32)
            for k in range(7):
                total = total + self.rc[b, k].astype(F32)
            self.db[b, core] = total.astype(BF16)
            self.copy(core, b, 12).start()

        self.place.each_core(step)

    def finish(self, b, out):
        def step(core):
            slot = self.db.at[b, 1 - core]
            send(slot, slot, self.ss.at[b, 12], self.rs.at[b, 12], self.place.at(flip_c=True)).wait_recv()
            for k in range(16):
                self.copy(core, b, k).wait_send()
            for half in (0, 1):
                mine = self.db[b, half].astype(F32)[core * 56 : core * 56 + 56]
                out[:, b * 256 + half * 128 : b * 256 + half * 128 + 128] = mine.astype(BF16)

        self.place.each_core(step)


def kernel(
    th_hbm, tw_hbm, hid, sw_hbm, tok, mask, loss_out, out,
    th, tw, sw, ht, pair, et, es, gb, info, tcol, col, coef, hold, ex, lossv, pb, rp, ra, rb, mid, rc, db,
    local_sem, pair_sems, ex_send, ex_recv, g_send, g_recv, r_send, r_recv, st_send, st_recv, s_send, s_recv,
):
    place = Place()
    across = {"rows": 1 - place.row}
    peers = place.peers() + [across]
    barrier = pltpu.get_barrier_semaphore()
    for peer in peers:
        pl.semaphore_signal(barrier, inc=1, device_id=peer, device_id_type=pl.DeviceIdType.MESH)

    th_load = lambda i: pltpu.make_async_copy(th_hbm.at[pl.ds(i * 128, 128)], th.at[pl.ds(i * 128, 128)], local_sem.at[i])
    tw_load = lambda i: pltpu.make_async_copy(
        tw_hbm.at[pl.ds(i * 1024, 1024)], tw.at[pl.ds(i * 1024, 1024)], local_sem.at[6 + i]
    )
    sw_load = lambda i: pltpu.make_async_copy(
        sw_hbm.at[pl.ds(i * 896, 896)], sw.at[pl.ds(i * 896, 896)], local_sem.at[10 + i]
    )
    th_load(0).start()
    for i in range(4):
        tw_load(i).start()
    for i in range(1, 6):
        th_load(i).start()
    for i in range(4):
        sw_load(i).start()

    mine = jnp.concatenate([hid[...].astype(F32), jnp.zeros((8, 768), F32)], axis=0).astype(BF16)
    for b in range(3):
        for half in (0, 1):
            pair[0, b, half] = mine[:, b * 256 + half * 128 : b * 256 + half * 128 + 128]
    pl.semaphore_wait(barrier, len(peers))
    swaps = [
        send(
            pair.at[0, b, 1 - place.c], pair.at[1, b, 1 - place.c], pair_sems.at[0, b], pair_sems.at[1, b], place.at(flip_c=True)
        )
        for b in range(3)
    ]
    for swap in swaps:
        swap.start()

    weights = mask[...].astype(F32).reshape(1, 768)
    ex[0] = jnp.broadcast_to(jnp.sum(weights, axis=1, keepdims=True), (8, 128))
    count = send(ex.at[0], ex.at[1], ex_send.at[0], ex_recv.at[0], across)
    gather = Gather(place, ht, g_send, g_recv, r_send, r_recv)

    for b in range(3):
        slot = pair.at[1, b, place.c]
        send(slot, slot, pair_sems.at[0, b], pair_sems.at[1, b], place.at(flip_c=True)).wait_recv()
        own = pair[0, b, place.c].astype(F32)[:56]
        theirs = pair[1, b, place.c].astype(F32)[:56]
        first = place.c == 0
        both = jnp.concatenate([jnp.where(first, own, theirs), jnp.where(first, theirs, own)], axis=0)
        ht[2 * b + place.c, place.x, place.z, place.y] = both.astype(BF16)
        gather.first(b)

    count.start()
    first_col = lax.axis_index("vocab") * 1280
    local_tok = (tok[...] - first_col).astype(F32).reshape(1, 768)
    info[...] = jnp.broadcast_to(local_tok, (128, 768)).T

    for b in range(3):
        gather.line(b)
    for i in range(4):
        tw_load(i).wait()

    def teacher(i, carry):
        rows = pl.ds(pl.multiple_of(i * 128, 128), 128)
        th_load(i).wait()
        et[rows, :] = jnp.dot(th[rows, :], tw[...], preferred_element_type=F32)

        @pl.when(i == 1)
        def _():
            gather.plane(0)
            gather.plane_rest(0)

        pl.when(i == 2)(lambda: gather.plane(1))

        @pl.when(i == 3)
        def _():
            gather.onward(0)
            gather.plane_rest(1)
            gather.plane(2)

        pl.when(i == 4)(lambda: gather.rest(0))

        @pl.when(i == 5)
        def _():
            gather.onward(1)
            gather.plane_rest(2)

        return carry

    lax.fori_loop(0, 6, teacher, None)

    lane = lax.broadcasted_iota(jnp.int32, (STRIP, 128), 1)
    strips = [slice(j * 128, j * 128 + 128) for j in range(10)]

    def strip(i):
        return pl.ds(pl.multiple_of(i * STRIP, STRIP), STRIP)

    def row_max(ref, rows):
        top = functools.reduce(jnp.maximum, [ref[rows, j] for j in strips])
        return jnp.max(top, axis=1, keepdims=True)

    def row_sum(value):
        return jnp.sum(value, axis=1, keepdims=True)

    def teacher_rows(i, carry):
        rows = strip(i)
        top = row_max(et, rows)
        total = mean = jnp.zeros((STRIP, 128), F32)
        for j in strips:
            t = et[rows, j]
            e = jnp.exp(t - top)
            et[rows, j] = e
            total, mean = total + e, mean + e * t
        tcol[rows, :] = jnp.where(
            lane == 0, top, jnp.where(lane == 1, row_sum(total), jnp.where(lane == 2, row_sum(mean), 0.0))
        )
        return carry

    lax.fori_loop(0, 6, teacher_rows, None)
    gather.rest(1)
    lax.fori_loop(6, 12, teacher_rows, None)
    for i in range(4):
        sw_load(i).wait()
    count.wait()

    stats = Statistics(place, hold, st_send, st_recv)
    column = lax.broadcasted_iota(jnp.int32, (STRIP, 128), 1).astype(F32)

    def student_rows(b):
        def step(i, carry):
            rows = strip(b * 4 + i)
            top = row_max(es, rows)
            token = info[rows, :]
            total = mean = target = jnp.zeros((STRIP, 128), F32)
            for j in strips:
                s = es[rows, j]
                e = jnp.exp(s - top)
                es[rows, j] = e
                total, mean = total + e, mean + et[rows, j] * s
                target = target + jnp.where(column == token - j.start, s, 0.0)
            old = tcol[rows, :]
            new = jnp.where(lane == 2, old - row_sum(mean), old)
            new = jnp.where(lane == 3, top, jnp.where(lane == 4, row_sum(total), jnp.where(lane == 5, row_sum(target), new)))
            col[strip(i), :] = new
            return carry

        lax.fori_loop(0, 4, step, None)
        stats.start(b, 0, col[...].T[:8])

    def settle(b):
        total = stats.total(b, 1)
        mine = hold[b, 0, stats.own(0)]
        t_lse = total[0:1] + jnp.log(total[1:2])
        s_lse = total[3:4] + jnp.log(total[4:5])
        row_kl = total[2:3] / total[1:2] - t_lse + s_lse
        row_nll = s_lse - total[5:6]
        masked = ex[0, 0:1, 0:1] + ex[1, 0:1, 0:1]
        weight = lossv[b, 1:2]
        lossv[b, 0:1] = weight * (row_kl + CE_WEIGHT * row_nll)
        scale = weight / masked
        a_s = (1.0 + CE_WEIGHT) * scale * jnp.exp(mine[3:4] - s_lse)
        a_t = scale * jnp.exp(mine[0:1] - t_lse)
        a_o = CE_WEIGHT * scale
        rows = jnp.concatenate([a_s, a_t, a_o, a_o, a_o, a_o, a_o, a_o], axis=0)
        coef[b] = jnp.concatenate([rows] * 16, axis=0).T

    for b in range(3):
        lossv[b, 1:2] = weights[:, b * 256 : b * 256 + 256]

    def student(b, carry):
        pl.when(b == 0)(lambda: gather.onward(2))
        pl.when(b == 1)(lambda: gather.rest(2))
        gather.whole(b)
        lhs = jnp.concatenate([ht[2 * b].reshape(3584, 128), ht[2 * b + 1].reshape(3584, 128)], axis=1)
        es[pl.ds(pl.multiple_of(b * 256, 256), 256), :] = lax.dot_general(
            lhs, sw[...], (((0,), (0,)), ((), ())), preferred_element_type=F32
        )
        student_rows(b)
        pl.when(b >= 1)(lambda: stats.start(b - 1, 1, stats.total(b - 1, 0)))
        pl.when(b == 2)(lambda: settle(0))
        return carry

    lax.fori_loop(0, 3, student, None)

    scatter = Scatter(place, pb, (rp, ra, rb, mid, rc, db), s_send, s_recv)

    def grad_rows(b):
        def step(i, carry):
            rows, full = strip(i), strip(b * 4 + i)
            token = info[full, :]
            a_s, a_t, a_o = (jnp.broadcast_to(coef[b, rows, k : k + 1], (STRIP, 128)) for k in range(3))
            for j in strips:
                chosen = jnp.where(column == token - j.start, a_o, 0.0)
                gb[rows, j] = (es[full, j] * a_s - et[full, j] * a_t - chosen).astype(BF16)
            return carry

        lax.fori_loop(0, 4, step, None)

    def backward(i, carry):
        b, half = i // 2, i % 2
        pl.when(half == 0)(lambda: grad_rows(b))
        part = lax.dot_general(
            sw[pl.ds(pl.multiple_of(half * 1792, 1792), 1792), :],
            gb[...],
            (((1,), (1,)), ((), ())),
            preferred_element_type=F32,
        ).astype(BF16)
        pb[b, 0, pl.ds(half * 2, 2)] = part[:, :128].reshape(2, 4, 2, 112, 128)
        pb[b, 1, pl.ds(half * 2, 2)] = part[:, 128:].reshape(2, 4, 2, 112, 128)
        pl.when(half == 0)(lambda: scatter.start_pair(b, 0))
        pl.when(half == 1)(lambda: scatter.start_pair(b, 1))

        @pl.when(i == 1)
        def _():
            stats.start(2, 1, stats.total(2, 0))
            settle(1)

        pl.when(i == 2)(lambda: scatter.lead_far(0))
        pl.when(i == 3)(lambda: settle(2))

        @pl.when(i == 4)
        def _():
            scatter.lead_far(1)
            scatter.lead_near(0)

        return carry

    lax.fori_loop(0, 6, backward, None)
    part = lossv[0, 0:1] + lossv[1, 0:1] + lossv[2, 0:1]
    ex[2] = jnp.broadcast_to(jnp.sum(part, axis=1, keepdims=True), (8, 128))
    loss = send(ex.at[2], ex.at[3], ex_send.at[1], ex_recv.at[1], across)
    loss.start()
    scatter.lead_far(2)
    scatter.lead_near(1)
    scatter.second(0)
    scatter.lead_near(2)
    scatter.second(1)
    scatter.last(0)
    scatter.second(2)
    scatter.last(1)
    scatter.finish(0, out)
    scatter.last(2)
    scatter.finish(1, out)
    loss.wait()
    loss_out[...] = (ex[2] + ex[3]) / (ex[0] + ex[1])

    def tidy(b, carry):
        gather.drain(b)
        stats.drain(b)
        return carry

    lax.fori_loop(0, 3, tidy, None)
    for swap in swaps:
        swap.wait_send()
    scatter.finish(2, out)


def results_kernel(loss, grad, loss_out, grad_out):
    loss_out[0, 0] = loss[0, 0]
    grad_out[...] = grad[...]


def local(teacher_hidden, teacher_head, student_hidden, student_head, token_ids, response_mask):
    loss, grad = pl.pallas_call(
        kernel,
        out_shape=(jax.ShapeDtypeStruct((8, 128), F32), jax.ShapeDtypeStruct((56, 768), BF16)),
        in_specs=[ANY, ANY, VMEM, ANY, VMEM, VMEM],
        out_specs=(VMEM, VMEM),
        scratch_shapes=[
            pltpu.VMEM((768, 4096), BF16),
            pltpu.VMEM((4096, 1280), BF16),
            pltpu.VMEM((3584, 1280), BF16),
            pltpu.VMEM((6, 4, 4, 2, 112, 128), BF16),
            pltpu.VMEM((2, 3, 2, 64, 128), BF16),
            pltpu.VMEM((768, 1280), F32),
            pltpu.VMEM((768, 1280), F32),
            pltpu.VMEM((256, 1280), BF16),
            pltpu.VMEM((768, 128), F32),
            pltpu.VMEM((768, 128), F32),
            pltpu.VMEM((256, 128), F32),
            pltpu.VMEM((3, 256, 128), F32),
            pltpu.VMEM((3, 2, 8, 8, 256), F32),
            pltpu.VMEM((4, 8, 128), F32),
            pltpu.VMEM((3, 8, 256), F32),
            pltpu.VMEM((3, 2, 4, 4, 2, 112, 128), BF16),
            pltpu.VMEM((3, 4, 4, 2, 112, 128), BF16),
            pltpu.VMEM((3, 2, 4, 112, 128), BF16),
            pltpu.VMEM((3, 2, 4, 2, 112, 128), BF16),
            pltpu.VMEM((3, 4, 2, 112, 128), BF16),
            pltpu.VMEM((3, 7, 112, 128), BF16),
            pltpu.VMEM((3, 2, 112, 128), BF16),
            DMA((14,)),
            DMA((2, 3)),
            DMA((2,)),
            DMA((2,)),
            DMA((3, 10)),
            DMA((3, 10)),
            DMA((3, 5)),
            DMA((3, 5)),
            DMA((3, 2, 7)),
            DMA((3, 2, 7)),
            DMA((3, 16)),
            DMA((3, 16)),
        ],
        compiler_params=pltpu.CompilerParams(collective_id=0, has_side_effects=True, vmem_limit_bytes=LIMIT),
        name="distill",
    )(teacher_hidden, teacher_head, student_hidden.T, student_head, token_ids, response_mask)
    loss, grad = pl.pallas_call(
        results_kernel,
        out_shape=(jax.ShapeDtypeStruct((1, 1), F32), jax.ShapeDtypeStruct((56, 768), BF16)),
        in_specs=[VMEM, VMEM],
        out_specs=(pl.BlockSpec(memory_space=pltpu.SMEM), VMEM),
        name="results",
    )(loss, grad)
    return loss[0, 0], grad.T


def solution(mesh):
    placed = (
        P("rows", None),
        P(None, "vocab"),
        P("rows", "vocab"),
        P(None, "vocab"),
        P("rows"),
        P("rows"),
    )
    return jax.shard_map(
        local, mesh=mesh, in_specs=placed, out_specs=(P(), P("rows", "vocab")), check_vma=False
    )
```

```python
import functools

import jax
import jax.numpy as jnp
from jax import lax
from jax.experimental import pallas as pl
from jax.experimental.pallas import tpu as pltpu
from jax.sharding import PartitionSpec as P

CE_WEIGHT = 0.5
STRIP = 64
F32, BF16 = jnp.float32, jnp.bfloat16
VMEM = pl.BlockSpec(memory_space=pltpu.VMEM)
ANY = pl.BlockSpec(memory_space=pl.ANY)
DMA = pltpu.SemaphoreType.DMA
LIMIT = 60 * 2**20


class Place:
    def __init__(self):
        v = lax.axis_index("vocab")
        self.x, self.z, self.y, self.c = v // 16, (v // 4) % 4, (v // 2) % 2, v % 2
        self.row = lax.axis_index("rows")

    def at(self, dx=0, dz=0, flip_y=False, flip_c=False):
        x, z = (self.x + dx) % 4, (self.z + dz) % 4
        y = 1 - self.y if flip_y else self.y
        c = 1 - self.c if flip_c else self.c
        return {"vocab": ((x * 4 + z) * 2 + y) * 2 + c}

    def peers(self):
        return (
            [self.at(dx=d, flip_y=f) for d in (1, 2, 3) for f in (False, True)]
            + [self.at(dz=d, flip_y=f) for d in (1, 2, 3) for f in (False, True)]
            + [self.at(dx=d, flip_c=True) for d in (1, 2, 3)]
            + self.square()
        )

    def square(self):
        return [self.at(flip_c=True), self.at(flip_y=True), self.at(flip_y=True, flip_c=True)]

    def each_core(self, step):
        for core in (0, 1):
            pl.when(self.c == core)(functools.partial(step, core))

    def lead(self, core, d, flip=False):
        return self.at(dx=d, flip_y=flip) if core == 0 else self.at(dz=d, flip_y=flip)

    def other(self, core, d, flip=False):
        return self.lead(1 - core, d, flip)

    def own(self, core):
        return (self.x, self.z) if core == 0 else (self.z, self.x)


def piece(ref, prefix, core, p, q, y):
    x, z = (p, q) if core == 0 else (q, p)
    return ref.at[(*prefix, x, z, y)]


def send(src, dst, send_sem, recv_sem, device):
    return pltpu.make_async_remote_copy(
        src_ref=src,
        dst_ref=dst,
        send_sem=send_sem,
        recv_sem=recv_sem,
        device_id=device,
        device_id_type=pl.DeviceIdType.MESH,
    )


ALL = slice(None)


SEVEN = ((1, False), (3, False), (0, True), (1, True), (3, True), (2, False), (2, True))


class Gather:
    def __init__(self, place, ht, send_sem, recv_sem, relay_send, relay_recv):
        self.place, self.ht = place, ht
        self.ss, self.rs, self.relay_ss, self.relay_rs = send_sem, recv_sem, relay_send, relay_recv

    def copy(self, core, b, k):
        place = self.place
        f, g = place.own(core)
        w = functools.partial(piece, self.ht, (2 * b + core,), core)
        src, device = [
            None,
            (w(f, g, ALL), place.lead(core, 1)),
            (w(f, g, ALL), place.lead(core, 2)),
            (w(f, g, ALL), place.lead(core, 3)),
            (w(ALL, g, 0), place.other(core, 1)),
            (w(ALL, g, 1), place.other(core, 3)),
            (w(ALL, g, 1), place.other(core, 1)),
            (w(ALL, g, 0), place.other(core, 3)),
            (w(ALL, (g + 3) % 4, 0), place.other(core, 1)),
            (w(ALL, (g + 1) % 4, 1), place.other(core, 3)),
        ][k]
        return send(src, src, self.ss.at[b, k], self.rs.at[b, k], device)

    def landed(self, core, b, k):
        f, g = self.place.own(core)
        w = functools.partial(piece, self.ht, (2 * b + core,), core)
        slot = [
            None,
            w((f + 3) % 4, g, ALL),
            w((f + 2) % 4, g, ALL),
            w((f + 1) % 4, g, ALL),
            w(ALL, (g + 3) % 4, 0),
            w(ALL, (g + 1) % 4, 1),
            w(ALL, (g + 3) % 4, 1),
            w(ALL, (g + 1) % 4, 0),
            w(ALL, (g + 2) % 4, 0),
            w(ALL, (g + 2) % 4, 1),
        ][k]
        send(slot, slot, self.ss.at[b, k], self.rs.at[b, k], self.place.at(flip_c=True)).wait_recv()

    def relay(self, core, b, k):
        f, g = self.place.own(core)
        w = functools.partial(piece, self.ht, (2 * b + core,), core)
        slot = [
            w(ALL, g, ALL),
            w(ALL, (g + 3) % 4, ALL),
            w(ALL, (g + 1) % 4, ALL),
            w(ALL, (g + 2) % 4, 0),
            w(ALL, (g + 2) % 4, 1),
        ][k]
        return send(slot, slot, self.relay_ss.at[b, k], self.relay_rs.at[b, k], self.place.at(flip_c=True))

    def line(self, b):
        def step(core):
            for k in (1, 3, 2):
                self.copy(core, b, k).start()

        self.place.each_core(step)

    def plane(self, b):
        def step(core):
            for k in (1, 2, 3):
                self.landed(core, b, k)
            self.copy(core, b, 4).start()
            self.copy(core, b, 5).start()
            self.relay(core, b, 0).start()

        self.place.each_core(step)

    def plane_rest(self, b):
        def step(core):
            self.copy(core, b, 6).start()
            self.copy(core, b, 7).start()

        self.place.each_core(step)

    def onward(self, b):
        def step(core):
            for k in (4, 5):
                self.landed(core, b, k)
                self.copy(core, b, k + 4).start()

        self.place.each_core(step)

    def rest(self, b):
        def step(core):
            for k in (6, 7):
                self.landed(core, b, k)
                self.relay(core, b, k - 5).start()

        self.place.each_core(step)

    def whole(self, b):
        def step(core):
            for k in (8, 9):
                self.landed(core, b, k)
                self.relay(core, b, k - 5).start()
            for k in range(5):
                self.relay(1 - core, b, k).wait_recv()

        self.place.each_core(step)

    def drain(self, b):
        def step(core):
            for k in range(1, 10):
                self.copy(core, b, k).wait_send()
            for k in range(5):
                self.relay(core, b, k).wait_send()

        self.place.each_core(step)


def merged(parts):
    t_max = functools.reduce(jnp.maximum, [p[0:1] for p in parts])
    s_max = functools.reduce(jnp.maximum, [p[3:4] for p in parts])
    t_w = [jnp.exp(p[0:1] - t_max) for p in parts]
    s_w = [jnp.exp(p[3:4] - s_max) for p in parts]
    t_sum = sum(w * p[1:2] for w, p in zip(t_w, parts))
    cross = sum(w * p[2:3] for w, p in zip(t_w, parts))
    s_sum = sum(w * p[4:5] for w, p in zip(s_w, parts))
    target = sum(p[5:6] for p in parts)
    return jnp.concatenate([t_max, t_sum, cross, s_max, s_sum, target, target, target], axis=0)


class Statistics:
    def __init__(self, place, hold, send_sem, recv_sem):
        self.place, self.hold, self.ss, self.rs = place, hold, send_sem, recv_sem

    def copies(self, b, stage):
        place = self.place
        own = self.own(stage)
        out = []
        for k, (d, flip) in enumerate(SEVEN):
            device = place.at(dx=d, flip_c=flip) if stage == 0 else place.at(dz=d, flip_y=flip)
            slot = self.hold.at[b, stage, own]
            out.append(send(slot, slot, self.ss.at[b, stage, k], self.rs.at[b, stage, k], device))
        return out

    def own(self, stage):
        place = self.place
        return place.x * 2 + place.c if stage == 0 else place.z * 2 + place.y

    def start(self, b, stage, value):
        self.hold[b, stage, self.own(stage)] = value
        for copy in self.copies(b, stage):
            copy.start()

    def total(self, b, stage):
        place = self.place
        main, pair = (place.x, place.c) if stage == 0 else (place.z, place.y)
        for k, (d, flip) in enumerate(SEVEN):
            index = (main + 4 - d) % 4 * 2 + (1 - pair if flip else pair)
            slot = self.hold.at[b, stage, index]
            send(slot, slot, self.ss.at[b, stage, k], self.rs.at[b, stage, k], place.at(flip_c=True)).wait_recv()
        return merged([self.hold[b, stage, i] for i in range(8)])

    def drain(self, b):
        for stage in (0, 1):
            for copy in self.copies(b, stage):
                copy.wait_send()


class Scatter:
    def __init__(self, place, pb, bufs, send_sem, recv_sem):
        self.place, self.pb = place, pb
        self.rp, self.ra, self.rb, self.mid, self.rc, self.db = bufs
        self.ss, self.rs = send_sem, recv_sem

    def copy(self, core, b, k):
        place = self.place
        f, g = place.own(core)
        w = functools.partial(piece, self.pb, (b, core), core)
        if 5 <= k < 12:
            d, flip = SEVEN[k - 5]
            src = self.mid.at[b, (g + d) % 4, 1 - place.y if flip else place.y]
            dst, device = self.rc.at[b, k - 5], place.other(core, d, flip)
        else:
            src, dst, device = {
                0: lambda: (self.pb.at[b, 1 - core, 0:2], self.rp.at[b, 0:2], place.at(flip_c=True)),
                13: lambda: (self.pb.at[b, 1 - core, 2:4], self.rp.at[b, 2:4], place.at(flip_c=True)),
                1: lambda: (w((f + 2) % 4, ALL, 0), self.ra.at[b, 0], place.lead(core, 1)),
                2: lambda: (w((f + 2) % 4, ALL, 1), self.ra.at[b, 1], place.lead(core, 3)),
                3: lambda: (w((f + 1) % 4, ALL, 1), self.rb.at[b, 0, :, 1], place.lead(core, 1)),
                4: lambda: (w((f + 3) % 4, ALL, 0), self.rb.at[b, 1, :, 0], place.lead(core, 3)),
                14: lambda: (w((f + 1) % 4, ALL, 0), self.rb.at[b, 0, :, 0], place.lead(core, 1)),
                15: lambda: (w((f + 3) % 4, ALL, 1), self.rb.at[b, 1, :, 1], place.lead(core, 3)),
                12: lambda: (self.db.at[b, core], self.db.at[b, core], place.at(flip_c=True)),
            }[k]()
        return send(src, dst, self.ss.at[b, k], self.rs.at[b, k], device)

    def start_pair(self, b, half):
        self.place.each_core(lambda core: self.copy(core, b, 13 * half).start())

    def pair_sum(self, core, b, ahead):
        f, g = self.place.own(core)
        at = piece(self.pb, (b, core), core, (f + ahead) % 4, ALL, ALL)
        theirs = piece(self.rp, (b,), core, (f + ahead) % 4, ALL, ALL)
        return at, at[...].astype(F32) + theirs[...].astype(F32)

    def lead_far(self, b):
        def step(core):
            self.copy(core, b, 0).wait_recv()
            self.copy(core, b, 13).wait_recv()
            for ahead in (2, 1, 3):
                at, value = self.pair_sum(core, b, ahead)
                at[...] = value.astype(BF16)
                for k in {2: (1, 2), 1: (3,), 3: (4,)}[ahead]:
                    self.copy(core, b, k).start()

        self.place.each_core(step)

    def lead_near(self, b):
        def step(core):
            f, g = self.place.own(core)
            for k, ahead, y in ((1, 1, 0), (2, 3, 1)):
                self.copy(core, b, k).wait_recv()
                at = piece(self.pb, (b, core), core, (f + ahead) % 4, ALL, y)
                at[...] = (at[...].astype(F32) + self.ra[b, k - 1].astype(F32)).astype(BF16)
                self.copy(core, b, k + 13).start()

        self.place.each_core(step)

    def second(self, b):
        def step(core):
            f, g = self.place.own(core)
            for k in (3, 4, 14, 15):
                self.copy(core, b, k).wait_recv()
            at, mine = self.pair_sum(core, b, 0)
            self.mid[b] = (mine + self.rb[b, 0].astype(F32) + self.rb[b, 1].astype(F32)).astype(BF16)
            for k in range(5, 12):
                self.copy(core, b, k).start()

        self.place.each_core(step)

    def last(self, b):
        def step(core):
            f, g = self.place.own(core)
            for k in range(5, 12):
                self.copy(core, b, k).wait_recv()
            total = self.mid.at[b, g, self.place.y][...].astype(F32)
            for k in range(7):
                total = total + self.rc[b, k].astype(F32)
            self.db[b, core] = total.astype(BF16)
            self.copy(core, b, 12).start()

        self.place.each_core(step)

    def finish(self, b, out):
        def step(core):
            slot = self.db.at[b, 1 - core]
            send(slot, slot, self.ss.at[b, 12], self.rs.at[b, 12], self.place.at(flip_c=True)).wait_recv()
            for k in range(16):
                self.copy(core, b, k).wait_send()
            for half in (0, 1):
                mine = self.db[b, half].astype(F32)[core * 56 : core * 56 + 56]
                out[:, b * 256 + half * 128 : b * 256 + half * 128 + 128] = mine.astype(BF16)

        self.place.each_core(step)


def kernel(
    th_hbm, tw_hbm, hid, sw_hbm, tok, mask, loss_out, out,
    th, tw, sw, ht, pair, near, et, es, gb, info, tcol, col, coef, hold, ex, lossv, pb, rp, ra, rb, mid, rc, db,
    local_sem, pair_sems, ex_send, ex_recv, g_send, g_recv, r_send, r_recv, st_send, st_recv, s_send, s_recv,
):
    place = Place()
    across = {"rows": 1 - place.row}
    peers = place.peers() + [across]
    barrier = pltpu.get_barrier_semaphore()
    for peer in peers:
        pl.semaphore_signal(barrier, inc=1, device_id=peer, device_id_type=pl.DeviceIdType.MESH)

    th_load = lambda i: pltpu.make_async_copy(th_hbm.at[pl.ds(i * 128, 128)], th.at[pl.ds(i * 128, 128)], local_sem.at[i])
    tw_load = lambda i: pltpu.make_async_copy(
        tw_hbm.at[pl.ds(i * 1024, 1024)], tw.at[pl.ds(i * 1024, 1024)], local_sem.at[6 + i]
    )
    sw_load = lambda i: pltpu.make_async_copy(
        sw_hbm.at[pl.ds(i * 896, 896)], sw.at[pl.ds(i * 896, 896)], local_sem.at[10 + i]
    )
    th_load(0).start()
    for i in range(4):
        tw_load(i).start()
    for i in range(1, 6):
        th_load(i).start()
    for i in range(4):
        sw_load(i).start()

    mine = jnp.concatenate([hid[...].astype(F32), jnp.zeros((8, 768), F32)], axis=0).astype(BF16)
    for b in range(3):
        for half in (0, 1):
            pair[b, half] = mine[:, b * 256 + half * 128 : b * 256 + half * 128 + 128]
    pl.semaphore_wait(barrier, len(peers))
    halves = [1 - place.c, place.c, 1 - place.c]
    swaps = [
        send(pair.at[b, halves[k]], near.at[k, b], pair_sems.at[0, k, b], pair_sems.at[1, k, b], device)
        for b in range(3)
        for k, device in enumerate(place.square())
    ]
    for swap in swaps:
        swap.start()

    weights = mask[...].astype(F32).reshape(1, 768)
    ex[0] = jnp.broadcast_to(jnp.sum(weights, axis=1, keepdims=True), (8, 128))
    count = send(ex.at[0], ex.at[1], ex_send.at[0], ex_recv.at[0], across)
    gather = Gather(place, ht, g_send, g_recv, r_send, r_recv)

    def joined(mine, theirs):
        mine, theirs = mine.astype(F32)[:56], theirs.astype(F32)[:56]
        first = place.c == 0
        return jnp.concatenate([jnp.where(first, mine, theirs), jnp.where(first, theirs, mine)], axis=0).astype(BF16)

    for b in range(3):
        for k in range(3):
            swaps[3 * b + k].wait_recv()
        ht[2 * b + place.c, place.x, place.z, place.y] = joined(pair[b, place.c], near[0, b])
        ht[2 * b + place.c, place.x, place.z, 1 - place.y] = joined(near[1, b], near[2, b])
        gather.line(b)
    count.start()
    first_col = lax.axis_index("vocab") * 1280
    local_tok = (tok[...] - first_col).astype(F32).reshape(1, 768)
    info[...] = jnp.broadcast_to(local_tok, (128, 768)).T

    for i in range(4):
        tw_load(i).wait()

    def teacher(i, carry):
        rows = pl.ds(pl.multiple_of(i * 128, 128), 128)
        th_load(i).wait()
        et[rows, :] = jnp.dot(th[rows, :], tw[...], preferred_element_type=F32)

        @pl.when(i == 1)
        def _():
            gather.plane(0)
            gather.plane_rest(0)

        pl.when(i == 2)(lambda: gather.plane(1))

        @pl.when(i == 3)
        def _():
            gather.onward(0)
            gather.plane_rest(1)
            gather.plane(2)

        pl.when(i == 4)(lambda: gather.rest(0))

        @pl.when(i == 5)
        def _():
            gather.onward(1)
            gather.plane_rest(2)

        return carry

    lax.fori_loop(0, 6, teacher, None)

    lane = lax.broadcasted_iota(jnp.int32, (STRIP, 128), 1)
    strips = [slice(j * 128, j * 128 + 128) for j in range(10)]

    def strip(i):
        return pl.ds(pl.multiple_of(i * STRIP, STRIP), STRIP)

    def row_max(ref, rows):
        top = functools.reduce(jnp.maximum, [ref[rows, j] for j in strips])
        return jnp.max(top, axis=1, keepdims=True)

    def row_sum(value):
        return jnp.sum(value, axis=1, keepdims=True)

    def teacher_rows(i, carry):
        rows = strip(i)
        top = row_max(et, rows)
        total = mean = jnp.zeros((STRIP, 128), F32)
        for j in strips:
            t = et[rows, j]
            e = jnp.exp(t - top)
            et[rows, j] = e
            total, mean = total + e, mean + e * t
        tcol[rows, :] = jnp.where(
            lane == 0, top, jnp.where(lane == 1, row_sum(total), jnp.where(lane == 2, row_sum(mean), 0.0))
        )
        return carry

    lax.fori_loop(0, 6, teacher_rows, None, unroll=2)
    gather.rest(1)
    lax.fori_loop(6, 12, teacher_rows, None, unroll=2)
    for i in range(4):
        sw_load(i).wait()
    count.wait()

    stats = Statistics(place, hold, st_send, st_recv)
    column = lax.broadcasted_iota(jnp.int32, (STRIP, 128), 1).astype(F32)

    def student_rows(b):
        def step(i, carry):
            rows = strip(b * 4 + i)
            top = row_max(es, rows)
            token = info[rows, :]
            total = mean = target = jnp.zeros((STRIP, 128), F32)
            for j in strips:
                s = es[rows, j]
                e = jnp.exp(s - top)
                es[rows, j] = e
                total, mean = total + e, mean + et[rows, j] * s
                target = target + jnp.where(column == token - j.start, s, 0.0)
            old = tcol[rows, :]
            new = jnp.where(lane == 2, old - row_sum(mean), old)
            new = jnp.where(lane == 3, top, jnp.where(lane == 4, row_sum(total), jnp.where(lane == 5, row_sum(target), new)))
            col[strip(i), :] = new
            return carry

        lax.fori_loop(0, 4, step, None, unroll=True)
        stats.start(b, 0, col[...].T[:8])

    def settle(b):
        total = stats.total(b, 1)
        mine = hold[b, 0, stats.own(0)]
        t_lse = total[0:1] + jnp.log(total[1:2])
        s_lse = total[3:4] + jnp.log(total[4:5])
        row_kl = total[2:3] / total[1:2] - t_lse + s_lse
        row_nll = s_lse - total[5:6]
        masked = ex[0, 0:1, 0:1] + ex[1, 0:1, 0:1]
        weight = lossv[b, 1:2]
        lossv[b, 0:1] = weight * (row_kl + CE_WEIGHT * row_nll)
        scale = weight / masked
        a_s = (1.0 + CE_WEIGHT) * scale * jnp.exp(mine[3:4] - s_lse)
        a_t = scale * jnp.exp(mine[0:1] - t_lse)
        a_o = CE_WEIGHT * scale
        rows = jnp.concatenate([a_s, a_t, a_o, a_o, a_o, a_o, a_o, a_o], axis=0)
        coef[b] = jnp.concatenate([rows] * 16, axis=0).T

    for b in range(3):
        lossv[b, 1:2] = weights[:, b * 256 : b * 256 + 256]

    def student(b, carry):
        pl.when(b == 0)(lambda: gather.onward(2))
        pl.when(b == 1)(lambda: gather.rest(2))
        gather.whole(b)
        lhs = jnp.concatenate([ht[2 * b].reshape(3584, 128), ht[2 * b + 1].reshape(3584, 128)], axis=1)
        es[pl.ds(pl.multiple_of(b * 256, 256), 256), :] = lax.dot_general(
            lhs, sw[...], (((0,), (0,)), ((), ())), preferred_element_type=F32
        )
        student_rows(b)
        pl.when(b >= 1)(lambda: stats.start(b - 1, 1, stats.total(b - 1, 0)))
        pl.when(b == 2)(lambda: settle(0))
        return carry

    lax.fori_loop(0, 3, student, None)

    scatter = Scatter(place, pb, (rp, ra, rb, mid, rc, db), s_send, s_recv)

    def grad_rows(b):
        def step(i, carry):
            rows, full = strip(i), strip(b * 4 + i)
            token = info[full, :]
            a_s, a_t, a_o = (jnp.broadcast_to(coef[b, rows, k : k + 1], (STRIP, 128)) for k in range(3))
            for j in strips:
                chosen = jnp.where(column == token - j.start, a_o, 0.0)
                gb[rows, j] = (es[full, j] * a_s - et[full, j] * a_t - chosen).astype(BF16)
            return carry

        lax.fori_loop(0, 4, step, None, unroll=True)

    def backward(i, carry):
        b, half = i // 2, i % 2
        pl.when(half == 0)(lambda: grad_rows(b))
        part = lax.dot_general(
            sw[pl.ds(pl.multiple_of(half * 1792, 1792), 1792), :],
            gb[...],
            (((1,), (1,)), ((), ())),
            preferred_element_type=F32,
        ).astype(BF16)
        pb[b, 0, pl.ds(half * 2, 2)] = part[:, :128].reshape(2, 4, 2, 112, 128)
        pb[b, 1, pl.ds(half * 2, 2)] = part[:, 128:].reshape(2, 4, 2, 112, 128)
        pl.when(half == 0)(lambda: scatter.start_pair(b, 0))
        pl.when(half == 1)(lambda: scatter.start_pair(b, 1))

        @pl.when(i == 1)
        def _():
            stats.start(2, 1, stats.total(2, 0))
            settle(1)

        pl.when(i == 2)(lambda: scatter.lead_far(0))
        pl.when(i == 3)(lambda: settle(2))

        @pl.when(i == 4)
        def _():
            scatter.lead_far(1)
            scatter.lead_near(0)

        return carry

    lax.fori_loop(0, 6, backward, None)
    part = lossv[0, 0:1] + lossv[1, 0:1] + lossv[2, 0:1]
    ex[2] = jnp.broadcast_to(jnp.sum(part, axis=1, keepdims=True), (8, 128))
    loss = send(ex.at[2], ex.at[3], ex_send.at[1], ex_recv.at[1], across)
    loss.start()
    scatter.lead_far(2)
    scatter.lead_near(1)
    scatter.second(0)
    scatter.lead_near(2)
    scatter.second(1)
    scatter.last(0)
    scatter.second(2)
    scatter.last(1)
    scatter.finish(0, out)
    scatter.last(2)
    scatter.finish(1, out)
    loss.wait()
    loss_out[...] = (ex[2] + ex[3]) / (ex[0] + ex[1])

    def tidy(b, carry):
        gather.drain(b)
        stats.drain(b)
        return carry

    lax.fori_loop(0, 3, tidy, None)
    for swap in swaps:
        swap.wait_send()
    scatter.finish(2, out)


def results_kernel(loss, grad, loss_out, grad_out):
    loss_out[0, 0] = loss[0, 0]
    grad_out[...] = grad[...]


def local(teacher_hidden, teacher_head, student_hidden, student_head, token_ids, response_mask):
    loss, grad = pl.pallas_call(
        kernel,
        out_shape=(jax.ShapeDtypeStruct((8, 128), F32), jax.ShapeDtypeStruct((56, 768), BF16)),
        in_specs=[ANY, ANY, VMEM, ANY, VMEM, VMEM],
        out_specs=(VMEM, VMEM),
        scratch_shapes=[
            pltpu.VMEM((768, 4096), BF16),
            pltpu.VMEM((4096, 1280), BF16),
            pltpu.VMEM((3584, 1280), BF16),
            pltpu.VMEM((6, 4, 4, 2, 112, 128), BF16),
            pltpu.VMEM((3, 2, 64, 128), BF16),
            pltpu.VMEM((3, 3, 64, 128), BF16),
            pltpu.VMEM((768, 1280), F32),
            pltpu.VMEM((768, 1280), F32),
            pltpu.VMEM((256, 1280), BF16),
            pltpu.VMEM((768, 128), F32),
            pltpu.VMEM((768, 128), F32),
            pltpu.VMEM((256, 128), F32),
            pltpu.VMEM((3, 256, 128), F32),
            pltpu.VMEM((3, 2, 8, 8, 256), F32),
            pltpu.VMEM((4, 8, 128), F32),
            pltpu.VMEM((3, 8, 256), F32),
            pltpu.VMEM((3, 2, 4, 4, 2, 112, 128), BF16),
            pltpu.VMEM((3, 4, 4, 2, 112, 128), BF16),
            pltpu.VMEM((3, 2, 4, 112, 128), BF16),
            pltpu.VMEM((3, 2, 4, 2, 112, 128), BF16),
            pltpu.VMEM((3, 4, 2, 112, 128), BF16),
            pltpu.VMEM((3, 7, 112, 128), BF16),
            pltpu.VMEM((3, 2, 112, 128), BF16),
            DMA((14,)),
            DMA((2, 3, 3)),
            DMA((2,)),
            DMA((2,)),
            DMA((3, 10)),
            DMA((3, 10)),
            DMA((3, 5)),
            DMA((3, 5)),
            DMA((3, 2, 7)),
            DMA((3, 2, 7)),
            DMA((3, 16)),
            DMA((3, 16)),
        ],
        compiler_params=pltpu.CompilerParams(collective_id=0, has_side_effects=True, vmem_limit_bytes=LIMIT),
        name="distill",
    )(teacher_hidden, teacher_head, student_hidden.T, student_head, token_ids, response_mask)
    loss, grad = pl.pallas_call(
        results_kernel,
        out_shape=(jax.ShapeDtypeStruct((1, 1), F32), jax.ShapeDtypeStruct((56, 768), BF16)),
        in_specs=[VMEM, VMEM],
        out_specs=(pl.BlockSpec(memory_space=pltpu.SMEM), VMEM),
        name="results",
    )(loss, grad)
    return loss[0, 0], grad.T


def solution(mesh):
    placed = (
        P("rows", None),
        P(None, "vocab"),
        P("rows", "vocab"),
        P(None, "vocab"),
        P("rows"),
        P("rows"),
    )
    return jax.shard_map(
        local, mesh=mesh, in_specs=placed, out_specs=(P(), P("rows", "vocab")), check_vma=False
    )
```

```python
import functools

import jax
import jax.numpy as jnp
from jax import lax
from jax.experimental import pallas as pl
from jax.experimental.pallas import tpu as pltpu
from jax.sharding import PartitionSpec as P

CE_WEIGHT = 0.5
STRIP = 128
F32, BF16 = jnp.float32, jnp.bfloat16
VMEM = pl.BlockSpec(memory_space=pltpu.VMEM)
ANY = pl.BlockSpec(memory_space=pl.ANY)
DMA = pltpu.SemaphoreType.DMA
LIMIT = 60 * 2**20


class Place:
    def __init__(self):
        v = lax.axis_index("vocab")
        self.x, self.z, self.y, self.c = v // 16, (v // 4) % 4, (v // 2) % 2, v % 2
        self.row = lax.axis_index("rows")

    def at(self, dx=0, dz=0, flip_y=False, flip_c=False):
        x, z = (self.x + dx) % 4, (self.z + dz) % 4
        y = 1 - self.y if flip_y else self.y
        c = 1 - self.c if flip_c else self.c
        return {"vocab": ((x * 4 + z) * 2 + y) * 2 + c}

    def peers(self):
        return (
            [self.at(dx=d, flip_y=f) for d in (1, 2, 3) for f in (False, True)]
            + [self.at(dz=d, flip_y=f) for d in (1, 2, 3) for f in (False, True)]
            + [self.at(dx=d, flip_c=True) for d in (1, 2, 3)]
            + self.square()
        )

    def square(self):
        return [self.at(flip_c=True), self.at(flip_y=True), self.at(flip_y=True, flip_c=True)]

    def each_core(self, step):
        for core in (0, 1):
            pl.when(self.c == core)(functools.partial(step, core))

    def lead(self, core, d, flip=False):
        return self.at(dx=d, flip_y=flip) if core == 0 else self.at(dz=d, flip_y=flip)

    def other(self, core, d, flip=False):
        return self.lead(1 - core, d, flip)

    def own(self, core):
        return (self.x, self.z) if core == 0 else (self.z, self.x)


def piece(ref, prefix, core, p, q, y):
    x, z = (p, q) if core == 0 else (q, p)
    return ref.at[(*prefix, x, z, y)]


def send(src, dst, send_sem, recv_sem, device):
    return pltpu.make_async_remote_copy(
        src_ref=src,
        dst_ref=dst,
        send_sem=send_sem,
        recv_sem=recv_sem,
        device_id=device,
        device_id_type=pl.DeviceIdType.MESH,
    )


ALL = slice(None)


SEVEN = ((1, False), (3, False), (0, True), (1, True), (3, True), (2, False), (2, True))


class Gather:
    def __init__(self, place, ht, send_sem, recv_sem, relay_send, relay_recv):
        self.place, self.ht = place, ht
        self.ss, self.rs, self.relay_ss, self.relay_rs = send_sem, recv_sem, relay_send, relay_recv

    def copy(self, core, b, k):
        place = self.place
        f, g = place.own(core)
        w = functools.partial(piece, self.ht, (2 * b + core,), core)
        src, device = [
            None,
            (w(f, g, ALL), place.lead(core, 1)),
            (w(f, g, ALL), place.lead(core, 2)),
            (w(f, g, ALL), place.lead(core, 3)),
            (w(ALL, g, 0), place.other(core, 1)),
            (w(ALL, g, 1), place.other(core, 3)),
            (w(ALL, g, 1), place.other(core, 1)),
            (w(ALL, g, 0), place.other(core, 3)),
            (w(ALL, (g + 3) % 4, 0), place.other(core, 1)),
            (w(ALL, (g + 1) % 4, 1), place.other(core, 3)),
        ][k]
        return send(src, src, self.ss.at[b, k], self.rs.at[b, k], device)

    def landed(self, core, b, k):
        f, g = self.place.own(core)
        w = functools.partial(piece, self.ht, (2 * b + core,), core)
        slot = [
            None,
            w((f + 3) % 4, g, ALL),
            w((f + 2) % 4, g, ALL),
            w((f + 1) % 4, g, ALL),
            w(ALL, (g + 3) % 4, 0),
            w(ALL, (g + 1) % 4, 1),
            w(ALL, (g + 3) % 4, 1),
            w(ALL, (g + 1) % 4, 0),
            w(ALL, (g + 2) % 4, 0),
            w(ALL, (g + 2) % 4, 1),
        ][k]
        send(slot, slot, self.ss.at[b, k], self.rs.at[b, k], self.place.at(flip_c=True)).wait_recv()

    def relay(self, core, b, k):
        f, g = self.place.own(core)
        w = functools.partial(piece, self.ht, (2 * b + core,), core)
        slot = [
            w(ALL, g, ALL),
            w(ALL, (g + 3) % 4, ALL),
            w(ALL, (g + 1) % 4, ALL),
            w(ALL, (g + 2) % 4, 0),
            w(ALL, (g + 2) % 4, 1),
        ][k]
        return send(slot, slot, self.relay_ss.at[b, k], self.relay_rs.at[b, k], self.place.at(flip_c=True))

    def line(self, b):
        def step(core):
            for k in (1, 3, 2):
                self.copy(core, b, k).start()

        self.place.each_core(step)

    def plane(self, b):
        def step(core):
            for k in (1, 2, 3):
                self.landed(core, b, k)
            self.copy(core, b, 4).start()
            self.copy(core, b, 5).start()
            self.relay(core, b, 0).start()

        self.place.each_core(step)

    def plane_rest(self, b):
        def step(core):
            self.copy(core, b, 6).start()
            self.copy(core, b, 7).start()

        self.place.each_core(step)

    def onward(self, b):
        def step(core):
            for k in (4, 5):
                self.landed(core, b, k)
                self.copy(core, b, k + 4).start()

        self.place.each_core(step)

    def rest(self, b):
        def step(core):
            for k in (6, 7):
                self.landed(core, b, k)
                self.relay(core, b, k - 5).start()

        self.place.each_core(step)

    def whole(self, b):
        def step(core):
            for k in (8, 9):
                self.landed(core, b, k)
                self.relay(core, b, k - 5).start()
            for k in range(5):
                self.relay(1 - core, b, k).wait_recv()

        self.place.each_core(step)

    def drain(self, b):
        def step(core):
            for k in range(1, 10):
                self.copy(core, b, k).wait_send()
            for k in range(5):
                self.relay(core, b, k).wait_send()

        self.place.each_core(step)


def merged(parts):
    t_max = functools.reduce(jnp.maximum, [p[0:1] for p in parts])
    s_max = functools.reduce(jnp.maximum, [p[3:4] for p in parts])
    t_w = [jnp.exp(p[0:1] - t_max) for p in parts]
    s_w = [jnp.exp(p[3:4] - s_max) for p in parts]
    t_sum = sum(w * p[1:2] for w, p in zip(t_w, parts))
    cross = sum(w * p[2:3] for w, p in zip(t_w, parts))
    s_sum = sum(w * p[4:5] for w, p in zip(s_w, parts))
    target = sum(p[5:6] for p in parts)
    return jnp.concatenate([t_max, t_sum, cross, s_max, s_sum, target, target, target], axis=0)


class Statistics:
    def __init__(self, place, hold, send_sem, recv_sem):
        self.place, self.hold, self.ss, self.rs = place, hold, send_sem, recv_sem

    def copies(self, b, stage):
        place = self.place
        own = self.own(stage)
        out = []
        for k, (d, flip) in enumerate(SEVEN):
            device = place.at(dx=d, flip_c=flip) if stage == 0 else place.at(dz=d, flip_y=flip)
            slot = self.hold.at[b, stage, own]
            out.append(send(slot, slot, self.ss.at[b, stage, k], self.rs.at[b, stage, k], device))
        return out

    def own(self, stage):
        place = self.place
        return place.x * 2 + place.c if stage == 0 else place.z * 2 + place.y

    def start(self, b, stage, value):
        self.hold[b, stage, self.own(stage)] = value
        for copy in self.copies(b, stage):
            copy.start()

    def total(self, b, stage):
        place = self.place
        main, pair = (place.x, place.c) if stage == 0 else (place.z, place.y)
        for k, (d, flip) in enumerate(SEVEN):
            index = (main + 4 - d) % 4 * 2 + (1 - pair if flip else pair)
            slot = self.hold.at[b, stage, index]
            send(slot, slot, self.ss.at[b, stage, k], self.rs.at[b, stage, k], place.at(flip_c=True)).wait_recv()
        return merged([self.hold[b, stage, i] for i in range(8)])

    def drain(self, b):
        for stage in (0, 1):
            for copy in self.copies(b, stage):
                copy.wait_send()


class Scatter:
    def __init__(self, place, pb, bufs, send_sem, recv_sem):
        self.place, self.pb = place, pb
        self.rp, self.ra, self.rb, self.mid, self.rc, self.db = bufs
        self.ss, self.rs = send_sem, recv_sem

    def copy(self, core, b, k):
        place = self.place
        f, g = place.own(core)
        w = functools.partial(piece, self.pb, (b, core), core)
        if 5 <= k < 12:
            d, flip = SEVEN[k - 5]
            src = self.mid.at[b, (g + d) % 4, 1 - place.y if flip else place.y]
            dst, device = self.rc.at[b, k - 5], place.other(core, d, flip)
        else:
            src, dst, device = {
                0: lambda: (self.pb.at[b, 1 - core, 0:2], self.rp.at[b, 0:2], place.at(flip_c=True)),
                13: lambda: (self.pb.at[b, 1 - core, 2:4], self.rp.at[b, 2:4], place.at(flip_c=True)),
                1: lambda: (w((f + 2) % 4, ALL, 0), self.ra.at[b, 0], place.lead(core, 1)),
                2: lambda: (w((f + 2) % 4, ALL, 1), self.ra.at[b, 1], place.lead(core, 3)),
                3: lambda: (w((f + 1) % 4, ALL, 1), self.rb.at[b, 0, :, 1], place.lead(core, 1)),
                4: lambda: (w((f + 3) % 4, ALL, 0), self.rb.at[b, 1, :, 0], place.lead(core, 3)),
                14: lambda: (w((f + 1) % 4, ALL, 0), self.rb.at[b, 0, :, 0], place.lead(core, 1)),
                15: lambda: (w((f + 3) % 4, ALL, 1), self.rb.at[b, 1, :, 1], place.lead(core, 3)),
                12: lambda: (self.db.at[b, core], self.db.at[b, core], place.at(flip_c=True)),
            }[k]()
        return send(src, dst, self.ss.at[b, k], self.rs.at[b, k], device)

    def start_pair(self, b, half):
        self.place.each_core(lambda core: self.copy(core, b, 13 * half).start())

    def pair_sum(self, core, b, ahead):
        f, g = self.place.own(core)
        at = piece(self.pb, (b, core), core, (f + ahead) % 4, ALL, ALL)
        theirs = piece(self.rp, (b,), core, (f + ahead) % 4, ALL, ALL)
        return at, at[...].astype(F32) + theirs[...].astype(F32)

    def lead_far(self, b):
        def step(core):
            self.copy(core, b, 0).wait_recv()
            self.copy(core, b, 13).wait_recv()
            for ahead in (2, 1, 3):
                at, value = self.pair_sum(core, b, ahead)
                at[...] = value.astype(BF16)
                for k in {2: (1, 2), 1: (3,), 3: (4,)}[ahead]:
                    self.copy(core, b, k).start()

        self.place.each_core(step)

    def lead_near(self, b):
        def step(core):
            f, g = self.place.own(core)
            for k, ahead, y in ((1, 1, 0), (2, 3, 1)):
                self.copy(core, b, k).wait_recv()
                at = piece(self.pb, (b, core), core, (f + ahead) % 4, ALL, y)
                at[...] = (at[...].astype(F32) + self.ra[b, k - 1].astype(F32)).astype(BF16)
                self.copy(core, b, k + 13).start()

        self.place.each_core(step)

    def second(self, b):
        def step(core):
            f, g = self.place.own(core)
            for k in (3, 4, 14, 15):
                self.copy(core, b, k).wait_recv()
            mine = piece(self.pb, (b, core), core, f, ALL, ALL)
            theirs = piece(self.rp, (b,), core, f, ALL, ALL)
            for d, ks in ((2, (10, 11)), (1, (5, 8)), (3, (6, 9)), (0, (7,))):
                to = (g + d) % 4
                parts = (mine[to], theirs[to], self.rb[b, 0, to], self.rb[b, 1, to])
                self.mid[b, to] = sum(part.astype(F32) for part in parts).astype(BF16)
                for k in ks:
                    self.copy(core, b, k).start()

        self.place.each_core(step)

    def last(self, b):
        def step(core):
            f, g = self.place.own(core)
            for k in range(5, 12):
                self.copy(core, b, k).wait_recv()
            total = self.mid.at[b, g, self.place.y][...].astype(F32)
            for k in range(7):
                total = total + self.rc[b, k].astype(F32)
            self.db[b, core] = total.astype(BF16)
            self.copy(core, b, 12).start()

        self.place.each_core(step)

    def finish(self, b, out):
        def step(core):
            slot = self.db.at[b, 1 - core]
            send(slot, slot, self.ss.at[b, 12], self.rs.at[b, 12], self.place.at(flip_c=True)).wait_recv()
            for k in range(16):
                self.copy(core, b, k).wait_send()
            for half in (0, 1):
                mine = self.db[b, half].astype(F32)[core * 56 : core * 56 + 56]
                out[:, b * 256 + half * 128 : b * 256 + half * 128 + 128] = mine.astype(BF16)

        self.place.each_core(step)


def kernel(
    th_hbm, tw_hbm, hid, sw_hbm, tok, mask, loss_out, out,
    th, tw, sw, ht, pair, near, et, es, gb, info, tcol, col, coef, hold, ex, lossv, pb, rp, ra, rb, mid, rc, db,
    local_sem, pair_sems, ex_send, ex_recv, g_send, g_recv, r_send, r_recv, st_send, st_recv, s_send, s_recv,
):
    place = Place()
    across = {"rows": 1 - place.row}
    peers = place.peers() + [across]
    barrier = pltpu.get_barrier_semaphore()
    for peer in peers:
        pl.semaphore_signal(barrier, inc=1, device_id=peer, device_id_type=pl.DeviceIdType.MESH)

    th_load = lambda i: pltpu.make_async_copy(th_hbm.at[pl.ds(i * 128, 128)], th.at[pl.ds(i * 128, 128)], local_sem.at[i])
    tw_load = lambda i: pltpu.make_async_copy(
        tw_hbm.at[pl.ds(i * 1024, 1024)], tw.at[pl.ds(i * 1024, 1024)], local_sem.at[6 + i]
    )
    sw_load = lambda i: pltpu.make_async_copy(
        sw_hbm.at[pl.ds(i * 896, 896)], sw.at[pl.ds(i * 896, 896)], local_sem.at[10 + i]
    )
    th_load(0).start()
    for i in range(4):
        tw_load(i).start()
    for i in range(1, 6):
        th_load(i).start()
    for i in range(4):
        sw_load(i).start()

    mine = jnp.concatenate([hid[...].astype(F32), jnp.zeros((8, 768), F32)], axis=0).astype(BF16)
    for b in range(3):
        for half in (0, 1):
            pair[b, half] = mine[:, b * 256 + half * 128 : b * 256 + half * 128 + 128]
    pl.semaphore_wait(barrier, len(peers))
    halves = [1 - place.c, place.c, 1 - place.c]
    swaps = [
        send(pair.at[b, halves[k]], near.at[k, b], pair_sems.at[0, k, b], pair_sems.at[1, k, b], device)
        for b in range(3)
        for k, device in enumerate(place.square())
    ]
    for swap in swaps:
        swap.start()

    weights = mask[...].astype(F32).reshape(1, 768)
    ex[0] = jnp.broadcast_to(jnp.sum(weights, axis=1, keepdims=True), (8, 128))
    count = send(ex.at[0], ex.at[1], ex_send.at[0], ex_recv.at[0], across)
    gather = Gather(place, ht, g_send, g_recv, r_send, r_recv)

    def joined(mine, theirs):
        mine, theirs = mine.astype(F32)[:56], theirs.astype(F32)[:56]
        first = place.c == 0
        return jnp.concatenate([jnp.where(first, mine, theirs), jnp.where(first, theirs, mine)], axis=0).astype(BF16)

    for b in range(3):
        for k in range(3):
            swaps[3 * b + k].wait_recv()
        ht[2 * b + place.c, place.x, place.z, place.y] = joined(pair[b, place.c], near[0, b])
        ht[2 * b + place.c, place.x, place.z, 1 - place.y] = joined(near[1, b], near[2, b])
        gather.line(b)
    count.start()
    first_col = lax.axis_index("vocab") * 1280
    local_tok = (tok[...] - first_col).astype(F32).reshape(1, 768)
    info[...] = jnp.broadcast_to(local_tok, (128, 768)).T

    for i in range(4):
        tw_load(i).wait()

    def teacher(i, carry):
        rows = pl.ds(pl.multiple_of(i * 128, 128), 128)
        th_load(i).wait()
        et[rows, :] = jnp.dot(th[rows, :], tw[...], preferred_element_type=F32)

        @pl.when(i == 1)
        def _():
            gather.plane(0)
            gather.plane_rest(0)

        pl.when(i == 2)(lambda: gather.plane(1))

        @pl.when(i == 3)
        def _():
            gather.onward(0)
            gather.plane_rest(1)
            gather.plane(2)

        pl.when(i == 4)(lambda: gather.rest(0))

        @pl.when(i == 5)
        def _():
            gather.onward(1)
            gather.plane_rest(2)

        return carry

    lax.fori_loop(0, 6, teacher, None)

    lane = lax.broadcasted_iota(jnp.int32, (STRIP, 128), 1)
    strips = [slice(j * 128, j * 128 + 128) for j in range(10)]

    def strip(i):
        return pl.ds(pl.multiple_of(i * STRIP, STRIP), STRIP)

    def row_max(ref, rows):
        top = functools.reduce(jnp.maximum, [ref[rows, j] for j in strips])
        return jnp.max(top, axis=1, keepdims=True)

    def row_sum(value):
        return jnp.sum(value, axis=1, keepdims=True)

    def teacher_rows(i, carry):
        rows = strip(i)
        top = row_max(et, rows)
        total = mean = jnp.zeros((STRIP, 128), F32)
        for j in strips:
            t = et[rows, j]
            e = jnp.exp(t - top)
            et[rows, j] = e
            total, mean = total + e, mean + e * t
        tcol[rows, :] = jnp.where(
            lane == 0, top, jnp.where(lane == 1, row_sum(total), jnp.where(lane == 2, row_sum(mean), 0.0))
        )
        return carry

    lax.fori_loop(0, 3, teacher_rows, None)
    gather.rest(1)
    lax.fori_loop(3, 6, teacher_rows, None)
    for i in range(4):
        sw_load(i).wait()
    count.wait()

    stats = Statistics(place, hold, st_send, st_recv)
    column = lax.broadcasted_iota(jnp.int32, (STRIP, 128), 1).astype(F32)

    def student_rows(b):
        def step(i, carry):
            rows = strip(b * 2 + i)
            top = row_max(es, rows)
            token = info[rows, :]
            total = mean = target = jnp.zeros((STRIP, 128), F32)
            for j in strips:
                s = es[rows, j]
                e = jnp.exp(s - top)
                es[rows, j] = e
                total, mean = total + e, mean + et[rows, j] * s
                target = target + jnp.where(column == token - j.start, s, 0.0)
            old = tcol[rows, :]
            new = jnp.where(lane == 2, old - row_sum(mean), old)
            new = jnp.where(lane == 3, top, jnp.where(lane == 4, row_sum(total), jnp.where(lane == 5, row_sum(target), new)))
            col[strip(i), :] = new
            return carry

        lax.fori_loop(0, 2, step, None, unroll=True)
        stats.start(b, 0, col[...].T[:8])

    def settle(b):
        total = stats.total(b, 1)
        mine = hold[b, 0, stats.own(0)]
        t_lse = total[0:1] + jnp.log(total[1:2])
        s_lse = total[3:4] + jnp.log(total[4:5])
        row_kl = total[2:3] / total[1:2] - t_lse + s_lse
        row_nll = s_lse - total[5:6]
        masked = ex[0, 0:1, 0:1] + ex[1, 0:1, 0:1]
        weight = lossv[b, 1:2]
        lossv[b, 0:1] = weight * (row_kl + CE_WEIGHT * row_nll)
        scale = weight / masked
        a_s = (1.0 + CE_WEIGHT) * scale * jnp.exp(mine[3:4] - s_lse)
        a_t = scale * jnp.exp(mine[0:1] - t_lse)
        a_o = CE_WEIGHT * scale
        rows = jnp.concatenate([a_s, a_t, a_o, a_o, a_o, a_o, a_o, a_o], axis=0)
        coef[b] = jnp.concatenate([rows] * 16, axis=0).T

    for b in range(3):
        lossv[b, 1:2] = weights[:, b * 256 : b * 256 + 256]

    def student(b, carry):
        gather.whole(b)
        lhs = jnp.concatenate([ht[2 * b].reshape(3584, 128), ht[2 * b + 1].reshape(3584, 128)], axis=1)
        es[pl.ds(pl.multiple_of(b * 256, 256), 256), :] = lax.dot_general(
            lhs, sw[...], (((0,), (0,)), ((), ())), preferred_element_type=F32
        )
        pl.when(b == 0)(lambda: gather.onward(2))
        student_rows(b)
        pl.when(b == 0)(lambda: gather.rest(2))
        pl.when(b >= 1)(lambda: stats.start(b - 1, 1, stats.total(b - 1, 0)))
        pl.when(b == 2)(lambda: settle(0))
        return carry

    lax.fori_loop(0, 3, student, None)

    scatter = Scatter(place, pb, (rp, ra, rb, mid, rc, db), s_send, s_recv)

    def grad_rows(b):
        def step(i, carry):
            rows, full = strip(i), strip(b * 2 + i)
            token = info[full, :]
            a_s, a_t, a_o = (jnp.broadcast_to(coef[b, rows, k : k + 1], (STRIP, 128)) for k in range(3))
            for j in strips:
                chosen = jnp.where(column == token - j.start, a_o, 0.0)
                gb[rows, j] = (es[full, j] * a_s - et[full, j] * a_t - chosen).astype(BF16)
            return carry

        lax.fori_loop(0, 2, step, None, unroll=True)

    def backward(i, carry):
        b, half = i // 2, i % 2
        pl.when(half == 0)(lambda: grad_rows(b))
        part = lax.dot_general(
            sw[pl.ds(pl.multiple_of(half * 1792, 1792), 1792), :],
            gb[...],
            (((1,), (1,)), ((), ())),
            preferred_element_type=F32,
        ).astype(BF16)
        pb[b, 0, pl.ds(half * 2, 2)] = part[:, :128].reshape(2, 4, 2, 112, 128)
        pb[b, 1, pl.ds(half * 2, 2)] = part[:, 128:].reshape(2, 4, 2, 112, 128)
        pl.when(half == 0)(lambda: scatter.start_pair(b, 0))
        pl.when(half == 1)(lambda: scatter.start_pair(b, 1))

        @pl.when(i == 1)
        def _():
            stats.start(2, 1, stats.total(2, 0))
            settle(1)

        pl.when(i == 2)(lambda: scatter.lead_far(0))
        pl.when(i == 3)(lambda: settle(2))

        @pl.when(i == 4)
        def _():
            scatter.lead_far(1)
            scatter.lead_near(0)

        return carry

    lax.fori_loop(0, 6, backward, None)
    part = lossv[0, 0:1] + lossv[1, 0:1] + lossv[2, 0:1]
    ex[2] = jnp.broadcast_to(jnp.sum(part, axis=1, keepdims=True), (8, 128))
    loss = send(ex.at[2], ex.at[3], ex_send.at[1], ex_recv.at[1], across)
    loss.start()
    scatter.lead_far(2)
    scatter.lead_near(1)
    scatter.second(0)
    scatter.lead_near(2)
    scatter.second(1)
    scatter.last(0)
    scatter.second(2)
    scatter.last(1)
    scatter.finish(0, out)
    scatter.last(2)
    scatter.finish(1, out)
    loss.wait()
    loss_out[...] = (ex[2] + ex[3]) / (ex[0] + ex[1])

    def tidy(b, carry):
        gather.drain(b)
        stats.drain(b)
        return carry

    lax.fori_loop(0, 3, tidy, None)
    for swap in swaps:
        swap.wait_send()
    scatter.finish(2, out)


def results_kernel(loss, grad, loss_out, grad_out):
    loss_out[0, 0] = loss[0, 0]
    grad_out[...] = grad[...]


def local(teacher_hidden, teacher_head, student_hidden, student_head, token_ids, response_mask):
    loss, grad = pl.pallas_call(
        kernel,
        out_shape=(jax.ShapeDtypeStruct((8, 128), F32), jax.ShapeDtypeStruct((56, 768), BF16)),
        in_specs=[ANY, ANY, VMEM, ANY, VMEM, VMEM],
        out_specs=(VMEM, VMEM),
        scratch_shapes=[
            pltpu.VMEM((768, 4096), BF16),
            pltpu.VMEM((4096, 1280), BF16),
            pltpu.VMEM((3584, 1280), BF16),
            pltpu.VMEM((6, 4, 4, 2, 112, 128), BF16),
            pltpu.VMEM((3, 2, 64, 128), BF16),
            pltpu.VMEM((3, 3, 64, 128), BF16),
            pltpu.VMEM((768, 1280), F32),
            pltpu.VMEM((768, 1280), F32),
            pltpu.VMEM((256, 1280), BF16),
            pltpu.VMEM((768, 128), F32),
            pltpu.VMEM((768, 128), F32),
            pltpu.VMEM((256, 128), F32),
            pltpu.VMEM((3, 256, 128), F32),
            pltpu.VMEM((3, 2, 8, 8, 256), F32),
            pltpu.VMEM((4, 8, 128), F32),
            pltpu.VMEM((3, 8, 256), F32),
            pltpu.VMEM((3, 2, 4, 4, 2, 112, 128), BF16),
            pltpu.VMEM((3, 4, 4, 2, 112, 128), BF16),
            pltpu.VMEM((3, 2, 4, 112, 128), BF16),
            pltpu.VMEM((3, 2, 4, 2, 112, 128), BF16),
            pltpu.VMEM((3, 4, 2, 112, 128), BF16),
            pltpu.VMEM((3, 7, 112, 128), BF16),
            pltpu.VMEM((3, 2, 112, 128), BF16),
            DMA((14,)),
            DMA((2, 3, 3)),
            DMA((2,)),
            DMA((2,)),
            DMA((3, 10)),
            DMA((3, 10)),
            DMA((3, 5)),
            DMA((3, 5)),
            DMA((3, 2, 7)),
            DMA((3, 2, 7)),
            DMA((3, 16)),
            DMA((3, 16)),
        ],
        compiler_params=pltpu.CompilerParams(collective_id=0, has_side_effects=True, vmem_limit_bytes=LIMIT),
        name="distill",
    )(teacher_hidden, teacher_head, student_hidden.T, student_head, token_ids, response_mask)
    loss, grad = pl.pallas_call(
        results_kernel,
        out_shape=(jax.ShapeDtypeStruct((1, 1), F32), jax.ShapeDtypeStruct((56, 768), BF16)),
        in_specs=[VMEM, VMEM],
        out_specs=(pl.BlockSpec(memory_space=pltpu.SMEM), VMEM),
        name="results",
    )(loss, grad)
    return loss[0, 0], grad.T


def solution(mesh):
    placed = (
        P("rows", None),
        P(None, "vocab"),
        P("rows", "vocab"),
        P(None, "vocab"),
        P("rows"),
        P("rows"),
    )
    return jax.shard_map(
        local, mesh=mesh, in_specs=placed, out_specs=(P(), P("rows", "vocab")), check_vma=False
    )
```
